32 devices in a mesh: gx: 4 (over z), gz: 2 (over x), ta: 4 (over y, core).
Axes of the slice: x: 2, y: 2, z: 4, core: 2. Of those that a mesh axis runs over, the one named last changes fastest.
Arguments:
- rhs: float32 [4, 2, 2, 8, 16, 8, 64], P('gx', None, None, 'gz', 'ta'), may hold values from -20 to 20
- self_coupling: bfloat16 [4, 2, 2, 8, 16, 64, 64], P('gx', None, None, 'gz', 'ta'), may hold values from -0.75 to 0.75
- hopping: bfloat16 [4, 4, 2, 2, 8, 16, 64, 64], P(None, 'gx', None, None, 'gz', 'ta'), may hold values from -0.5 to 0.5
Outputs:
- solution: float32 [4, 2, 2, 8, 16, 8, 64], P('gx', None, None, 'gz', 'ta')
- residual: float32 [4, 2, 2, 8, 16, 8, 64], P('gx', None, None, 'gz', 'ta')
The draws below stay inside these ranges and needn't reach their ends.
All inputs are finite; a program needn't handle non-finite values.
Results may differ from the reference program's by a relative error of at most 0.0087.
Values may be sent and summed in bfloat16 or wider, within the bound.
No kernel may reach another device: no remote copies, remote signals or barrier semaphores. Data moves between devices by JAX's collectives and lax.ppermute only.
A program may use at most 64 MiB of HBM per device.

```python
import jax
import jax.numpy as jnp
from jax import lax

C = 64
R = 8
BX = 2
BY = 2
BZ = 4
BT = 4
MR_STEPS = 2
NB = 4
PY = 2
LZ = 8
LT = 16


def draw_rhs(key, part):
    key_noise, key_spread = jax.random.split(key, 2)
    full_shape = (NB, BX, BY, LZ, LT, R, C)
    sample = jnp.clip(jax.random.normal(key_noise, full_shape, jnp.float32), -4.0, 4.0)
    spread = jax.random.uniform(key_spread, (NB, BX, BY, LZ, LT, 1, 1), jnp.float32, 0.0, 1.0)
    rising = jnp.arange(NB, dtype=jnp.float32).reshape(NB, 1, 1, 1, 1, 1, 1) / (NB - 1)
    factor = 10.0 ** spread * 3.0 ** rising / 6.0
    return sample * factor


def shard_levels(own_key, shape, cuts, low, top_value):
    def one(axis_at, blocks):
        heights = jax.random.uniform(jax.random.fold_in(jax.random.fold_in(own_key, 6), axis_at), (blocks,), jnp.float32, low / len(cuts), top_value / len(cuts))
        return jnp.repeat(jnp.exp(heights), shape[axis_at] // blocks).reshape((-1,) + (1,) * (len(shape) - axis_at - 1))

    gain = one(*cuts[0])
    for cut in cuts[1:]:
        gain = gain * one(*cut)
    return gain


def centred(rng, dims, deviation, reach, pieces=(), held_as=jnp.bfloat16):
    values = deviation * jax.random.normal(rng, dims, jnp.float32)
    if pieces:
        values = values * shard_levels(rng, dims, pieces, -0.22, 0.18)
    return jnp.clip(values, -reach, reach).astype(held_as)


def setup_inputs(seed: int = 0) -> dict:
    splits = jax.random.split(jax.random.key(seed), 4)
    return {
        "rhs": draw_rhs(jax.random.fold_in(splits[3], 71), 0),
        "self_coupling": centred(splits[1], (NB, BX, BY, LZ, LT, C, C), C ** -0.5, 0.75, ((0, 4), (3, 2), (4, 4))),
        "hopping": centred(splits[2], (4, NB, BX, BY, LZ, LT, C, C), (2 * C) ** -0.5, 0.5, ((1, 4), (4, 2), (5, 4))),
    }


forward_form = "xyztab,xyztrb->xyztra"
backward_form = "xyztab,xyztra->xyztrb"


def site_product(links, field_bf, form):
    def single(operands):
        return jnp.einsum(form, operands[0].astype(jnp.float32), operands[1].astype(jnp.float32))
    return lax.map(single, (links, field_bf))


def block_step(direction):
    return PY if direction == 0 else 1


def ahead_of(values, direction):
    if direction >= 2:
        return jnp.roll(values, -1, axis=direction + 1)
    axis = direction + 1
    extent = values.shape[axis]
    moved = jnp.roll(values, -block_step(direction), axis=0)
    inner = lax.slice_in_dim(values, 1, extent, axis=axis)
    edge = lax.slice_in_dim(moved, 0, 1, axis=axis)
    return jnp.concatenate([inner, edge], axis=axis)


def behind_of(values, direction):
    if direction >= 2:
        return jnp.roll(values, 1, axis=direction + 1)
    axis = direction + 1
    extent = values.shape[axis]
    moved = jnp.roll(values, block_step(direction), axis=0)
    inner = lax.slice_in_dim(values, 0, extent - 1, axis=axis)
    edge = lax.slice_in_dim(moved, extent - 1, extent, axis=axis)
    return jnp.concatenate([edge, inner], axis=axis)


def rim_masks():
    coords = [jnp.arange(BX).reshape(1, BX, 1, 1, 1, 1, 1),
              jnp.arange(BY).reshape(1, 1, BY, 1, 1, 1, 1),
              (jnp.arange(LZ) % BZ).reshape(1, 1, 1, LZ, 1, 1, 1),
              (jnp.arange(LT) % BT).reshape(1, 1, 1, 1, LT, 1, 1)]
    widths = [BX, BY, BZ, BT]
    upward = [(coords[direction] != widths[direction] - 1).astype(jnp.float32) for direction in range(4)]
    downward = [(coords[direction] != 0).astype(jnp.float32) for direction in range(4)]
    return upward, downward


def apply_operator(vector, self_coupling, hopping, confined):
    field_bf = vector.astype(jnp.bfloat16)
    chirality = jnp.where(jnp.arange(C) < C // 2, 1.0, -1.0).astype(jnp.bfloat16)
    result = 4.0 * vector + site_product(self_coupling, field_bf, forward_form)
    upward, downward = rim_masks()
    for direction in range(4):
        ahead_field = ahead_of(field_bf, direction)
        forward_term = site_product(hopping[direction], ahead_field, forward_form)
        back_term = (chirality * site_product(hopping[direction], chirality * field_bf, backward_form)).astype(jnp.bfloat16)
        behind = behind_of(back_term, direction).astype(jnp.float32)
        if confined:
            forward_term = forward_term * upward[direction]
            behind = behind * downward[direction]
        result = result + forward_term + behind
    return result


def mesh_dot(left, right):
    return jnp.sum(left * right, axis=(0, 1, 2, 3, 4, 6))[:, None]


def domain_ratio(mapped, remain):
    split_shape = (NB, BX, BY, LZ // BZ, BZ, LT // BT, BT, R, C)
    numer_sum = jnp.sum((mapped * remain).reshape(split_shape), axis=(1, 2, 4, 6, 8), keepdims=True)
    bottom = jnp.sum((mapped * mapped).reshape(split_shape), axis=(1, 2, 4, 6, 8), keepdims=True)
    return jnp.broadcast_to(numer_sum / bottom, split_shape).reshape(mapped.shape)


def smoothing(source, self_coupling, hopping):
    remain = source
    update = jnp.zeros_like(source)
    for repeat_index in range(MR_STEPS):
        mapped = apply_operator(remain, self_coupling, hopping, True)
        weight = domain_ratio(mapped, remain)
        update = update + weight * remain
        remain = remain - weight * mapped
    return update


def reference(rhs, self_coupling, hopping):
    direction_zero = smoothing(rhs, self_coupling, hopping)
    mapped_zero = apply_operator(direction_zero, self_coupling, hopping, False)
    norm_zero = mesh_dot(mapped_zero, mapped_zero)
    alpha_first = mesh_dot(mapped_zero, rhs) / norm_zero
    solution_one = alpha_first * direction_zero
    residual_one = rhs - alpha_first * mapped_zero
    direction_raw = smoothing(residual_one, self_coupling, hopping)
    mapped_raw = apply_operator(direction_raw, self_coupling, hopping, False)
    beta_value = mesh_dot(mapped_zero, mapped_raw) / norm_zero
    direction_one = direction_raw - beta_value * direction_zero
    mapped_one = mapped_raw - beta_value * mapped_zero
    alpha_second = mesh_dot(mapped_one, residual_one) / mesh_dot(mapped_one, mapped_one)
    solution = solution_one + alpha_second * direction_one
    residual = residual_one - alpha_second * mapped_one
    return solution, residual
```

```python
import functools

import jax
import jax.numpy as jnp
from jax import lax
from jax.experimental import pallas as pl
from jax.experimental.pallas import tpu as pltpu
from jax.sharding import PartitionSpec as P

F32 = jnp.float32
BF16 = jnp.bfloat16
NT = (((1,), (1,)), ((), ()))
NN = (((1,), (0,)), ((), ()))
VMEM_BYTES = 24 * 2**20
AXES = ("gx", "gx", "gz", "ta")


class Box:
    def __init__(self, extents):
        self.extents = tuple(extents)
        self.strides = []
        count = 1
        for extent in reversed(self.extents):
            self.strides.insert(0, count)
            count *= extent
        self.count = count

    def coord(self, site, direction):
        return site // self.strides[direction] % self.extents[direction]

    def ahead(self, site, direction):
        last = self.extents[direction] - 1
        return None if self.coord(site, direction) == last else site + self.strides[direction]

    def behind(self, site, direction):
        return None if self.coord(site, direction) == 0 else site - self.strides[direction]

    def rim(self, direction, upper):
        wanted = self.extents[direction] - 1 if upper else 0
        return [s for s in range(self.count) if self.coord(s, direction) == wanted]


def lane_tools(rows, lanes):
    lane = lax.broadcasted_iota(jnp.int32, (rows, lanes), 1)
    low = lane < lanes // 2
    chirality = jnp.where(lane % (lanes // 2) < lanes // 4, 1.0, -1.0).astype(F32)
    return low, chirality


def twice(value):
    return jnp.concatenate([value, value], axis=1)


def local_products(box, field, links, own, back, mapped, low, chirality):
    rows, lanes = field.shape[1:]
    half = lanes // 2
    zero = jnp.zeros((rows, lanes), F32)
    for s in range(box.count):
        ahead = [box.ahead(s, d) for d in range(4)]
        part = [zero if a is None else field[a] for a in ahead]
        here = field[s]
        spread = jnp.concatenate(
            [jnp.where(low, part[0], part[1]), jnp.where(low, part[2], part[3])], axis=1
        ).astype(BF16)
        total = lax.dot_general(here[:, :half].astype(BF16), own[s], NT, preferred_element_type=F32)
        if any(a is not None for a in ahead):
            total = total + lax.dot_general(spread, links[s], NT, preferred_element_type=F32)
        mapped[s] = jnp.concatenate([total, jnp.zeros((rows, half), F32)], axis=1)
        back[s] = lax.dot_general(
            (chirality * here)[:, :half].astype(BF16), links[s], NN, preferred_element_type=F32
        )
    top = zero
    bottom = zero
    for s in range(box.count):
        behind = [box.behind(s, d) for d in range(4)]
        piece = []
        for d in range(4):
            start = d // 2 * lanes
            piece.append(zero if behind[d] is None else back[behind[d], :, start : start + lanes])
        gathered = jnp.where(low, piece[0], piece[1]) + jnp.where(low, piece[2], piece[3])
        gathered = chirality * gathered + mapped[s]
        here = field[s]
        value = 4.0 * here + gathered + pltpu.roll(gathered, half, 1)
        mapped[s] = value
        top = top + value * here
        bottom = bottom + value * value
    return jnp.sum(top, axis=1, keepdims=True) / jnp.sum(bottom, axis=1, keepdims=True)


def smooth(box, flips, field, links, own, outs, scratch):
    update, image, sends = outs
    back_a, back_b, map_a, map_b, second = scratch
    rows, lanes = field.shape[1:]
    half = lanes // 2
    low, chirality = lane_tools(rows, lanes)
    weight_a = local_products(box, field, links, own, back_a, map_a, low, chirality)
    for s in range(box.count):
        second[s] = field[s] - weight_a * map_a[s]
    weight_b = local_products(box, second, links, own, back_b, map_b, low, chirality)
    for s in range(box.count):
        update[s] = weight_a * field[s] + weight_b * second[s]
        image[s] = weight_a * map_a[s] + weight_b * map_b[s]
    for d in range(4):
        flip = flips[d]
        lower = box.rim(d, False)
        upper = box.rim(d, True)
        start = d // 2 * lanes
        for j in range(len(lower) // 4):
            block = []
            for k in (4 * j, 4 * j + 2):
                block.append(jnp.where(low, update[lower[k]], update[lower[k + 1]]))
            sends[d][flip, j] = jnp.concatenate(block, axis=0).astype(BF16)
            block = []
            for k in (4 * j, 4 * j + 2):
                pair = []
                for u in (upper[k], upper[k + 1]):
                    pair.append(
                        weight_a * back_a[u, :, start : start + lanes]
                        + weight_b * back_b[u, :, start : start + lanes]
                    )
                if d % 2 == 0:
                    joined = jnp.where(low, pair[0], pltpu.roll(pair[1], half, 1))
                else:
                    joined = jnp.where(low, pltpu.roll(pair[0], half, 1), pair[1])
                block.append(chirality * joined)
            sends[d][1 - flip, j] = jnp.concatenate(block, axis=0).astype(BF16)


def first_kernel(box, flips, rhs, own, hop, update, image, send0, send1, send2, send3, links, field, *scratch):
    for s in range(box.count):
        links[s] = jnp.concatenate([hop[d, s] for d in range(4)], axis=1)
        field[s] = twice(rhs[s])
    smooth(box, flips, field, links, own, (update, image, (send0, send1, send2, send3)), scratch)


def second_kernel(box, flips, rhs, mapped, sums, links, own, update, image, send0, send1, send2, send3, field, *scratch):
    alpha = sums[:, 0:1] / sums[:, 1:2]
    for s in range(box.count):
        field[s] = twice(rhs[s]) - alpha * mapped[s]
    smooth(box, flips, field, links, own, (update, image, (send0, send1, send2, send3)), scratch)


def joined_halo(box, flips, image, links, came, mapped, low):
    rows, lanes = image.shape[1:]
    half = lanes // 2

    places = [{s: k for k, s in enumerate(box.rim(d, True))} for d in range(4)]
    lows = [{s: k for k, s in enumerate(box.rim(d, False))} for d in range(4)]

    def read(d, which, k):
        slot = flips[d] if which == 0 else 1 - flips[d]
        tile = came[d][slot, k // 4].astype(F32)
        tile = tile[(k // 2 % 2) * rows : (k // 2 % 2 + 1) * rows]
        if which == 0 and k % 2 != d % 2:
            tile = pltpu.roll(tile, half, 1)
        return tile

    zero = jnp.zeros((rows, lanes), F32)
    for s in range(box.count):
        part = [read(d, 0, places[d][s]) if s in places[d] else None for d in range(4)]
        extra = zero
        if any(p is not None for p in part):
            part = [zero if p is None else p for p in part]
            spread = jnp.concatenate(
                [jnp.where(low, part[0], part[1]), jnp.where(low, part[2], part[3])], axis=1
            ).astype(BF16)
            total = lax.dot_general(spread, links[s], NT, preferred_element_type=F32)
            extra = jnp.concatenate([total, jnp.zeros((rows, half), F32)], axis=1)
        for d in range(4):
            if s in lows[d]:
                k = lows[d][s]
                tile = read(d, 1, k)
                extra = extra + (jnp.where(low, tile, 0.0) if k % 2 == 0 else jnp.where(low, 0.0, tile))
        mapped[s] = image[s] + extra + pltpu.roll(extra, half, 1)


def packed_sums(values, rows, lanes):
    lane = lax.broadcasted_iota(jnp.int32, (rows, lanes), 1)
    out = jnp.zeros((rows, lanes), F32)
    for k, value in enumerate(values):
        out = jnp.where(lane == k, jnp.sum(value, axis=1, keepdims=True), out)
    return out


def third_kernel(box, flips, rhs, image, links, came0, came1, came2, came3, mapped, sums):
    rows, lanes = image.shape[1:]
    low, _ = lane_tools(rows, lanes)
    joined_halo(box, flips, image, links, (came0, came1, came2, came3), mapped, low)
    zero = jnp.zeros((rows, lanes), F32)
    top = zero
    bottom = zero
    for s in range(box.count):
        value = mapped[s]
        top = top + value * twice(rhs[s])
        bottom = bottom + value * value
    sums[...] = packed_sums((top, bottom), rows, lanes)


def fourth_kernel(box, flips, rhs, first, before, image, links, came0, came1, came2, came3, mapped, sums):
    rows, lanes = image.shape[1:]
    low, _ = lane_tools(rows, lanes)
    joined_halo(box, flips, image, links, (came0, came1, came2, came3), mapped, low)
    alpha = before[:, 0:1] / before[:, 1:2]
    total = [jnp.zeros((rows, lanes), F32) for _ in range(4)]
    for s in range(box.count):
        old = first[s]
        value = mapped[s]
        remain = twice(rhs[s]) - alpha * old
        for k, product in enumerate((old * value, value * value, value * remain, old * remain)):
            total[k] = total[k] + product
    sums[...] = packed_sums(total, rows, lanes)


def last_kernel(box, rhs, update_a, map_a, update_b, map_b, sums_a, sums_b, solution_out, residual_out):
    half = update_a.shape[2] // 2
    square = sums_a[:, 1:2]
    alpha = sums_a[:, 0:1] / square
    beta = sums_b[:, 0:1] / square
    top = sums_b[:, 2:3] - beta * sums_b[:, 3:4]
    bottom = sums_b[:, 1:2] - 2.0 * beta * sums_b[:, 0:1] + beta * beta * square
    step = top / bottom
    for s in range(box.count):
        old = update_a[s][:, :half]
        solution_out[s] = alpha * old + step * (update_b[s][:, :half] - beta * old)
        old = map_a[s][:, :half]
        residual_out[s] = rhs[s] - alpha * old - step * (map_b[s][:, :half] - beta * old)


def call(body, outs, scratch, ins, flips=None):
    vmem = pl.BlockSpec(memory_space=pltpu.VMEM)
    smem = pl.BlockSpec(memory_space=pltpu.SMEM)
    specs = [vmem] * len(ins)
    if flips is not None:
        specs.insert(0, smem)
        ins = (flips, *ins)
    return pl.pallas_call(
        body,
        out_shape=outs,
        in_specs=specs,
        out_specs=[vmem] * len(outs),
        scratch_shapes=scratch,
        compiler_params=pltpu.CompilerParams(vmem_limit_bytes=VMEM_BYTES),
    )(*ins)


def plan(direction):
    axis = AXES[direction]
    size = lax.axis_size(axis)
    step = min(8, max(2, lax.axis_size("gx") // 8)) if direction == 0 else 1
    if 2 * step % size == 0:
        return axis, size, step, "both"
    if step == 1 and size % 2 == 0:
        return axis, size, step, "pairs"
    return axis, size, step, "shift"


def exchange(sends):
    came = [None] * 4
    for d in range(4):
        axis, size, step, kind = plan(d)
        ring = range(size)
        if kind == "both":
            came[d] = lax.ppermute(sends[d], axis, [(i, (i + step) % size) for i in ring])
        elif kind == "pairs":
            even = lax.ppermute(sends[d][0], axis, [(i, i ^ 1) for i in ring])
            odd = lax.ppermute(sends[d][1], axis, [(i, (i + 1 if i % 2 else i - 1) % size) for i in ring])
            came[d] = jnp.stack([even, odd])
        else:
            field = lax.ppermute(sends[d][0], axis, [(i, (i - step) % size) for i in ring])
            back = lax.ppermute(sends[d][1], axis, [(i, (i + step) % size) for i in ring])
            came[d] = jnp.stack([field, back])
    return came


def mesh_sum(value):
    for axis in ("ta", "gz", "gx"):
        size = lax.axis_size(axis)
        if size & (size - 1):
            value = lax.psum(value, axis)
            continue
        hop = 1
        while hop < size:
            value = value + lax.ppermute(value, axis, [(i, i ^ hop) for i in range(size)])
            hop *= 2
    return value


def on_device(rhs, self_coupling, hopping):
    extents = rhs.shape[1:5]
    rows, channels = rhs.shape[5:]
    lanes = 2 * channels
    box = Box(extents)
    count = box.count
    source = rhs.reshape(count, rows, channels)
    own = self_coupling.reshape(count, channels, channels)
    hop = hopping.reshape(4, count, channels, channels)

    flips_out = []
    flips_in = []
    for d in range(4):
        axis, _, _, kind = plan(d)
        if kind == "pairs":
            odd = lax.axis_index(axis) % 2
            flips_out.append(1 - odd)
            flips_in.append(odd)
        else:
            flips_out.append(jnp.int32(0))
            flips_in.append(jnp.int32(0))
    flips_out = jnp.stack(flips_out).astype(jnp.int32)
    flips_in = jnp.stack(flips_in).astype(jnp.int32)

    full = jax.ShapeDtypeStruct((count, rows, lanes), F32)
    small = jax.ShapeDtypeStruct((rows, lanes), F32)
    narrow = jax.ShapeDtypeStruct((count, rows, channels), F32)
    links_shape = jax.ShapeDtypeStruct((count, channels, 4 * channels), BF16)
    send_shapes = [
        jax.ShapeDtypeStruct((2, len(box.rim(d, True)) // 4, 2 * rows, lanes), BF16) for d in range(4)
    ]
    field_scratch = pltpu.VMEM((count, rows, lanes), F32)
    back_scratch = pltpu.VMEM((count, rows, 4 * channels), F32)
    scratch = [field_scratch, back_scratch, back_scratch, field_scratch, field_scratch, field_scratch]

    update_a, image_a, *sends, links = call(
        functools.partial(first_kernel, box),
        [full, full, *send_shapes, links_shape],
        scratch,
        (source, own, hop),
        flips_out,
    )
    came = exchange(sends)
    map_a, sums_a = call(
        functools.partial(third_kernel, box), [full, small], [], (source, image_a, links, *came), flips_in
    )
    sums_a = mesh_sum(sums_a)
    update_b, image_b, *sends = call(
        functools.partial(second_kernel, box),
        [full, full, *send_shapes],
        scratch,
        (source, map_a, sums_a, links, own),
        flips_out,
    )
    came = exchange(sends)
    map_b, sums_b = call(
        functools.partial(fourth_kernel, box),
        [full, small],
        [],
        (source, map_a, sums_a, image_b, links, *came),
        flips_in,
    )
    sums_b = mesh_sum(sums_b)
    found, left = call(
        functools.partial(last_kernel, box),
        [narrow, narrow],
        [],
        (source, update_a, map_a, update_b, map_b, sums_a, sums_b),
    )
    return found.reshape(rhs.shape), left.reshape(rhs.shape)


def solution(mesh):
    in_specs = (
        P("gx", None, None, "gz", "ta", None, None),
        P("gx", None, None, "gz", "ta", None, None),
        P(None, "gx", None, None, "gz", "ta", None, None),
    )
    out_specs = (
        P("gx", None, None, "gz", "ta", None, None),
        P("gx", None, None, "gz", "ta", None, None),
    )
    return jax.shard_map(
        on_device, mesh=mesh, in_specs=in_specs, out_specs=out_specs, check_vma=False
    )
```

```python
import functools

import jax
import jax.numpy as jnp
from jax import lax
from jax.experimental import pallas as pl
from jax.experimental.pallas import tpu as pltpu
from jax.sharding import PartitionSpec as P

F32 = jnp.float32
BF16 = jnp.bfloat16
NT = (((1,), (1,)), ((), ()))
NN = (((1,), (0,)), ((), ()))
VMEM_BYTES = 24 * 2**20
GROUP = 4
AXES = ("gx", "gx", "gz", "ta")


class Box:
    def __init__(self, extents):
        self.extents = tuple(extents)
        self.strides = []
        count = 1
        for extent in reversed(self.extents):
            self.strides.insert(0, count)
            count *= extent
        self.count = count

    def coord(self, site, direction):
        return site // self.strides[direction] % self.extents[direction]

    def ahead(self, site, direction):
        last = self.extents[direction] - 1
        return None if self.coord(site, direction) == last else site + self.strides[direction]

    def behind(self, site, direction):
        return None if self.coord(site, direction) == 0 else site - self.strides[direction]

    def rim(self, direction, upper):
        wanted = self.extents[direction] - 1 if upper else 0
        return [s for s in range(self.count) if self.coord(s, direction) == wanted]


def lane_tools(rows, lanes):
    lane = lax.broadcasted_iota(jnp.int32, (rows, lanes), 1)
    low = lane < lanes // 2
    chirality = jnp.where(lane % (lanes // 2) < lanes // 4, 1.0, -1.0).astype(F32)
    return low, chirality


def twice(value):
    return jnp.concatenate([value, value], axis=1)


def own_products(group, here, own, low):
    rows, lanes = here[0].shape
    zero = jnp.zeros((rows, lanes), F32)
    left = [jnp.where(low, here[0], 0.0), jnp.where(low, 0.0, here[1]), zero, zero]
    right = [zero, zero, jnp.where(low, here[2], 0.0), jnp.where(low, 0.0, here[3])]
    blocks = jnp.concatenate(
        [jnp.concatenate(left, axis=0), jnp.concatenate(right, axis=0)], axis=1
    ).astype(BF16)
    return lax.dot_general(blocks, own[group], NT, preferred_element_type=F32)


def local_products(box, field, links, own, back, mapped, low, chirality, arrive=None):
    rows, lanes = field.shape[1:]
    half = lanes // 2
    zero = jnp.zeros((rows, lanes), F32)
    for g in range(box.count // GROUP):
        if arrive is not None:
            arrive(g)
        sites = range(GROUP * g, GROUP * g + GROUP)
        here = [field[s] for s in sites]
        diagonal = own_products(g, here, own, low)
        for i, s in enumerate(sites):
            ahead = [box.ahead(s, d) for d in range(4)]
            total = diagonal[i * rows : (i + 1) * rows]
            if any(a is not None for a in ahead):
                part = [zero if a is None else field[a] for a in ahead]
                spread = jnp.concatenate(
                    [jnp.where(low, part[0], part[1]), jnp.where(low, part[2], part[3])], axis=1
                ).astype(BF16)
                total = total + lax.dot_general(spread, links[s], NT, preferred_element_type=F32)
            mapped[s] = jnp.concatenate([total, jnp.zeros((rows, half), F32)], axis=1)
            back[s] = lax.dot_general(
                (chirality * here[i])[:, :half].astype(BF16),
                links[s],
                NN,
                preferred_element_type=F32,
            )
    top = zero
    bottom = zero
    for s in range(box.count):
        behind = [box.behind(s, d) for d in range(4)]
        piece = []
        for d in range(4):
            start = d // 2 * lanes
            piece.append(zero if behind[d] is None else back[behind[d], :, start : start + lanes])
        gathered = jnp.where(low, piece[0], piece[1]) + jnp.where(low, piece[2], piece[3])
        gathered = chirality * gathered + mapped[s]
        here = field[s]
        value = 4.0 * here + gathered + pltpu.roll(gathered, half, 1)
        mapped[s] = value
        top = top + value * here
        bottom = bottom + value * value
    return jnp.sum(top, axis=1, keepdims=True) / jnp.sum(bottom, axis=1, keepdims=True)


def smooth(box, flips, field, links, own, outs, scratch, arrive=None):
    update, image, sends = outs
    back_a, back_b, map_a, map_b, second = scratch
    rows, lanes = field.shape[1:]
    half = lanes // 2
    low, chirality = lane_tools(rows, lanes)
    weight_a = local_products(box, field, links, own, back_a, map_a, low, chirality, arrive)
    for s in range(box.count):
        second[s] = field[s] - weight_a * map_a[s]
    weight_b = local_products(box, second, links, own, back_b, map_b, low, chirality)
    for s in range(box.count):
        update[s] = weight_a * field[s] + weight_b * second[s]
        image[s] = weight_a * map_a[s] + weight_b * map_b[s]
    for d in range(4):
        flip = flips[d]
        lower = box.rim(d, False)
        upper = box.rim(d, True)
        start = d // 2 * lanes
        for j in range(len(lower) // 4):
            block = []
            for k in (4 * j, 4 * j + 2):
                block.append(jnp.where(low, update[lower[k]], update[lower[k + 1]]))
            sends[d][flip, j] = jnp.concatenate(block, axis=0).astype(BF16)
            block = []
            for k in (4 * j, 4 * j + 2):
                pair = []
                for u in (upper[k], upper[k + 1]):
                    pair.append(
                        weight_a * back_a[u, :, start : start + lanes]
                        + weight_b * back_b[u, :, start : start + lanes]
                    )
                if d % 2 == 0:
                    joined = jnp.where(low, pair[0], pltpu.roll(pair[1], half, 1))
                else:
                    joined = jnp.where(low, pltpu.roll(pair[0], half, 1), pair[1])
                block.append(chirality * joined)
            sends[d][1 - flip, j] = jnp.concatenate(block, axis=0).astype(BF16)


def first_kernel(
    box, parts, flips, rhs_in, own_in, hop_in, *refs
):
    update, image, send0, send1, send2, send3, links, own = refs[:8]
    field, back_a, back_b, map_a, map_b, second, rhs, own_raw, hop, sems = refs[8:]
    each = box.count // parts
    copies = [pltpu.make_async_copy(rhs_in, rhs, sems.at[2 * parts])]
    for c in range(parts):
        run = pl.ds(c * each, each)
        copies.append(pltpu.make_async_copy(hop_in.at[:, run], hop.at[:, run], sems.at[2 * c]))
        copies.append(pltpu.make_async_copy(own_in.at[run], own_raw.at[run], sems.at[2 * c + 1]))
    for copy in copies:
        copy.start()
    copies[0].wait()
    for s in range(box.count):
        field[s] = twice(rhs[s])

    def arrive(g):
        if g * GROUP % each == 0:
            c = g * GROUP // each
            copies[2 * c + 1].wait()
            copies[2 * c + 2].wait()
        sites = range(GROUP * g, GROUP * g + GROUP)
        own[g] = jnp.concatenate([own_raw[s] for s in sites], axis=1)
        for s in sites:
            links[s] = jnp.concatenate([hop[d, s] for d in range(4)], axis=1)

    scratch = (back_a, back_b, map_a, map_b, second)
    smooth(box, flips, field, links, own, (update, image, (send0, send1, send2, send3)), scratch, arrive)


def second_kernel(box, flips, rhs, mapped, sums, links, own, update, image, send0, send1, send2, send3, field, *scratch):
    top, square = unpacked_sums(sums, 2, mapped.shape[1])
    alpha = top / square
    for s in range(box.count):
        field[s] = twice(rhs[s]) - alpha * mapped[s]
    smooth(box, flips, field, links, own, (update, image, (send0, send1, send2, send3)), scratch)


def joined_halo(box, flips, image, links, came, mapped, low):
    rows, lanes = image.shape[1:]
    half = lanes // 2

    places = [{s: k for k, s in enumerate(box.rim(d, True))} for d in range(4)]
    lows = [{s: k for k, s in enumerate(box.rim(d, False))} for d in range(4)]

    def read(d, which, k):
        slot = flips[d] if which == 0 else 1 - flips[d]
        tile = came[d][slot, k // 4].astype(F32)
        tile = tile[(k // 2 % 2) * rows : (k // 2 % 2 + 1) * rows]
        if which == 0 and k % 2 != d % 2:
            tile = pltpu.roll(tile, half, 1)
        return tile

    zero = jnp.zeros((rows, lanes), F32)
    for s in range(box.count):
        part = [read(d, 0, places[d][s]) if s in places[d] else None for d in range(4)]
        extra = zero
        if any(p is not None for p in part):
            part = [zero if p is None else p for p in part]
            spread = jnp.concatenate(
                [jnp.where(low, part[0], part[1]), jnp.where(low, part[2], part[3])], axis=1
            ).astype(BF16)
            total = lax.dot_general(spread, links[s], NT, preferred_element_type=F32)
            extra = jnp.concatenate([total, jnp.zeros((rows, half), F32)], axis=1)
        for d in range(4):
            if s in lows[d]:
                k = lows[d][s]
                tile = read(d, 1, k)
                extra = extra + (jnp.where(low, tile, 0.0) if k % 2 == 0 else jnp.where(low, 0.0, tile))
        mapped[s] = image[s] + extra + pltpu.roll(extra, half, 1)


def sum_places(rows, lanes):
    row = lax.broadcasted_iota(jnp.int32, (rows, lanes), 0)
    lane = lax.broadcasted_iota(jnp.int32, (rows, lanes), 1)
    return lane - row


def packed_sums(values, out):
    rows, lanes = values[0].shape
    places = sum_places(rows, lanes)
    spread = jnp.zeros((rows, lanes), F32)
    for k, value in enumerate(values):
        spread = jnp.where(places == k * rows, jnp.sum(value, axis=1, keepdims=True), spread)
    out[...] = jnp.broadcast_to(jnp.sum(spread, axis=0, keepdims=True), out.shape)


def unpacked_sums(sums, count, rows):
    lanes = sums.shape[1]
    total = jnp.broadcast_to(jnp.sum(sums[...], axis=0, keepdims=True), (rows, lanes))
    places = sum_places(rows, lanes)
    return [
        jnp.sum(jnp.where(places == k * rows, total, 0.0), axis=1, keepdims=True) for k in range(count)
    ]


def third_kernel(box, flips, rhs, image, links, came3, came2, came1, came0, mapped, sums):
    rows, lanes = image.shape[1:]
    low, _ = lane_tools(rows, lanes)
    joined_halo(box, flips, image, links, (came0, came1, came2, came3), mapped, low)
    zero = jnp.zeros((rows, lanes), F32)
    top = zero
    bottom = zero
    for s in range(box.count):
        value = mapped[s]
        top = top + value * twice(rhs[s])
        bottom = bottom + value * value
    packed_sums((top, bottom), sums)


def fourth_kernel(box, flips, rhs, first, before, image, links, came3, came2, came1, came0, mapped, sums):
    rows, lanes = image.shape[1:]
    low, _ = lane_tools(rows, lanes)
    joined_halo(box, flips, image, links, (came0, came1, came2, came3), mapped, low)
    top, square = unpacked_sums(before, 2, rows)
    alpha = top / square
    total = [jnp.zeros((rows, lanes), F32) for _ in range(4)]
    for s in range(box.count):
        old = first[s]
        value = mapped[s]
        remain = twice(rhs[s]) - alpha * old
        for k, product in enumerate((old * value, value * value, value * remain, old * remain)):
            total[k] = total[k] + product
    packed_sums(total, sums)


def last_kernel(box, rhs, update_a, map_a, update_b, map_b, sums_a, sums_b, solution_out, residual_out):
    rows, lanes = update_a.shape[1:]
    half = lanes // 2
    top, square = unpacked_sums(sums_a, 2, rows)
    alpha = top / square
    cross, norm, raw, old = unpacked_sums(sums_b, 4, rows)
    beta = cross / square
    step = (raw - beta * old) / (norm - 2.0 * beta * cross + beta * beta * square)
    for s in range(box.count):
        old = update_a[s][:, :half]
        solution_out[s] = alpha * old + step * (update_b[s][:, :half] - beta * old)
        old = map_a[s][:, :half]
        residual_out[s] = rhs[s] - alpha * old - step * (map_b[s][:, :half] - beta * old)


def call(body, outs, scratch, ins, flips=None, space=pltpu.VMEM):
    vmem = pl.BlockSpec(memory_space=pltpu.VMEM)
    specs = [pl.BlockSpec(memory_space=space)] * len(ins)
    if flips is not None:
        specs.insert(0, pl.BlockSpec(memory_space=pltpu.SMEM))
        ins = (flips, *ins)
    return pl.pallas_call(
        body,
        out_shape=outs,
        in_specs=specs,
        out_specs=[vmem] * len(outs),
        scratch_shapes=scratch,
        compiler_params=pltpu.CompilerParams(vmem_limit_bytes=VMEM_BYTES),
    )(*ins)


def plan(direction):
    axis = AXES[direction]
    size = lax.axis_size(axis)
    step = min(8, max(2, lax.axis_size("gx") // 8)) if direction == 0 else 1
    if 2 * step % size == 0:
        return axis, size, step, "both"
    if step == 1 and size % 2 == 0:
        return axis, size, step, "pairs"
    return axis, size, step, "shift"


def exchange(sends):
    came = [None] * 4
    for d in reversed(range(4)):
        axis, size, step, kind = plan(d)
        ring = range(size)
        if kind == "both":
            came[d] = lax.ppermute(sends[d], axis, [(i, (i + step) % size) for i in ring])
        elif kind == "pairs":
            even = lax.ppermute(sends[d][0], axis, [(i, i ^ 1) for i in ring])
            odd = lax.ppermute(sends[d][1], axis, [(i, (i + 1 if i % 2 else i - 1) % size) for i in ring])
            came[d] = jnp.stack([even, odd])
        else:
            field = lax.ppermute(sends[d][0], axis, [(i, (i - step) % size) for i in ring])
            back = lax.ppermute(sends[d][1], axis, [(i, (i + step) % size) for i in ring])
            came[d] = jnp.stack([field, back])
    return came


def device_count():
    return lax.axis_size("gx") * lax.axis_size("gz") * lax.axis_size("ta")


def sum_rows():
    return device_count() if device_count() <= 64 else 1


def mesh_sum(value):
    if sum_rows() > 1:
        return lax.all_to_all(value, ("gx", "gz", "ta"), 0, 0, tiled=True)
    for axis in ("gx", "gz", "ta"):
        size = lax.axis_size(axis)
        if size & (size - 1):
            value = lax.psum(value, axis)
            continue
        hop = 1
        while hop < size:
            value = value + lax.ppermute(value, axis, [(i, i ^ hop) for i in range(size)])
            hop *= 2
    return value


def on_device(rhs, self_coupling, hopping):
    extents = rhs.shape[1:5]
    rows, channels = rhs.shape[5:]
    lanes = 2 * channels
    box = Box(extents)
    count = box.count
    source = rhs.reshape(count, rows, channels)
    own = self_coupling.reshape(count, channels, channels)
    hop = hopping.reshape(4, count, channels, channels)

    flips_out = []
    flips_in = []
    for d in range(4):
        axis, _, _, kind = plan(d)
        if kind == "pairs":
            odd = lax.axis_index(axis) % 2
            flips_out.append(1 - odd)
            flips_in.append(odd)
        else:
            flips_out.append(jnp.int32(0))
            flips_in.append(jnp.int32(0))
    flips_out = jnp.stack(flips_out).astype(jnp.int32)
    flips_in = jnp.stack(flips_in).astype(jnp.int32)

    full = jax.ShapeDtypeStruct((count, rows, lanes), F32)
    small = jax.ShapeDtypeStruct((sum_rows(), lanes), F32)
    narrow = jax.ShapeDtypeStruct((count, rows, channels), F32)
    links_shape = jax.ShapeDtypeStruct((count, channels, 4 * channels), BF16)
    own_shape = jax.ShapeDtypeStruct((count // GROUP, channels, GROUP * channels), BF16)
    parts = extents[0] * extents[1]
    raw = [
        pltpu.VMEM(source.shape, F32),
        pltpu.VMEM(own.shape, BF16),
        pltpu.VMEM(hop.shape, BF16),
        pltpu.SemaphoreType.DMA((2 * parts + 1,)),
    ]
    send_shapes = [
        jax.ShapeDtypeStruct((2, len(box.rim(d, True)) // 4, 2 * rows, lanes), BF16) for d in range(4)
    ]
    field_scratch = pltpu.VMEM((count, rows, lanes), F32)
    back_scratch = pltpu.VMEM((count, rows, 4 * channels), F32)
    scratch = [field_scratch, back_scratch, back_scratch, field_scratch, field_scratch, field_scratch]

    update_a, image_a, *sends, links, own = call(
        functools.partial(first_kernel, box, parts),
        [full, full, *send_shapes, links_shape, own_shape],
        scratch + raw,
        [pltpu.with_memory_space_constraint(a, pltpu.HBM) for a in (source, own, hop)],
        flips_out,
        pltpu.HBM,
    )
    came = exchange(sends)
    map_a, sums_a = call(
        functools.partial(third_kernel, box), [full, small], [], (source, image_a, links, *came[::-1]), flips_in
    )
    sums_a = mesh_sum(sums_a)
    update_b, image_b, *sends = call(
        functools.partial(second_kernel, box),
        [full, full, *send_shapes],
        scratch,
        (source, map_a, sums_a, links, own),
        flips_out,
    )
    came = exchange(sends)
    map_b, sums_b = call(
        functools.partial(fourth_kernel, box),
        [full, small],
        [],
        (source, map_a, sums_a, image_b, links, *came[::-1]),
        flips_in,
    )
    sums_b = mesh_sum(sums_b)
    found, left = call(
        functools.partial(last_kernel, box),
        [narrow, narrow],
        [],
        (source, update_a, map_a, update_b, map_b, sums_a, sums_b),
    )
    return found.reshape(rhs.shape), left.reshape(rhs.shape)


def solution(mesh):
    in_specs = (
        P("gx", None, None, "gz", "ta", None, None),
        P("gx", None, None, "gz", "ta", None, None),
        P(None, "gx", None, None, "gz", "ta", None, None),
    )
    out_specs = (
        P("gx", None, None, "gz", "ta", None, None),
        P("gx", None, None, "gz", "ta", None, None),
    )
    return jax.shard_map(
        on_device, mesh=mesh, in_specs=in_specs, out_specs=out_specs, check_vma=False
    )
```

```python
import functools

import jax
import jax.numpy as jnp
from jax import lax
from jax.experimental import pallas as pl
from jax.experimental.pallas import tpu as pltpu
from jax.sharding import PartitionSpec as P

F32 = jnp.float32
BF16 = jnp.bfloat16
NT = (((1,), (1,)), ((), ()))
NN = (((1,), (0,)), ((), ()))
VMEM_BYTES = 24 * 2**20
GROUP = 4
AXES = ("gx", "gx", "gz", "ta")


class Box:
    def __init__(self, extents):
        self.extents = tuple(extents)
        self.strides = []
        count = 1
        for extent in reversed(self.extents):
            self.strides.insert(0, count)
            count *= extent
        self.count = count

    def coord(self, site, direction):
        return site // self.strides[direction] % self.extents[direction]

    def ahead(self, site, direction):
        last = self.extents[direction] - 1
        return None if self.coord(site, direction) == last else site + self.strides[direction]

    def behind(self, site, direction):
        return None if self.coord(site, direction) == 0 else site - self.strides[direction]

    def rim(self, direction, upper):
        wanted = self.extents[direction] - 1 if upper else 0
        return [s for s in range(self.count) if self.coord(s, direction) == wanted]


def lane_tools(rows, lanes):
    lane = lax.broadcasted_iota(jnp.int32, (rows, lanes), 1)
    low = lane < lanes // 2
    chirality = jnp.where(lane % (lanes // 2) < lanes // 4, 1.0, -1.0).astype(F32)
    return low, chirality


def twice(value):
    return jnp.concatenate([value, value], axis=1)


def own_products(group, here, own, low):
    rows, lanes = here[0].shape
    zero = jnp.zeros((rows, lanes), F32)
    left = [jnp.where(low, here[0], 0.0), jnp.where(low, 0.0, here[1]), zero, zero]
    right = [zero, zero, jnp.where(low, here[2], 0.0), jnp.where(low, 0.0, here[3])]
    blocks = jnp.concatenate(
        [jnp.concatenate(left, axis=0), jnp.concatenate(right, axis=0)], axis=1
    ).astype(BF16)
    return lax.dot_general(blocks, own[group], NT, preferred_element_type=F32)


def local_products(box, field, links, own, back, mapped, low, chirality, arrive=None):
    rows, lanes = field.shape[1:]
    half = lanes // 2
    zero = jnp.zeros((rows, lanes), F32)
    for g in range(box.count // GROUP):
        if arrive is not None:
            arrive(g)
        sites = range(GROUP * g, GROUP * g + GROUP)
        here = [field[s] for s in sites]
        diagonal = own_products(g, here, own, low)
        for i, s in enumerate(sites):
            ahead = [box.ahead(s, d) for d in range(4)]
            total = diagonal[i * rows : (i + 1) * rows]
            if any(a is not None for a in ahead):
                part = [zero if a is None else field[a] for a in ahead]
                spread = jnp.concatenate(
                    [jnp.where(low, part[0], part[1]), jnp.where(low, part[2], part[3])], axis=1
                ).astype(BF16)
                total = total + lax.dot_general(spread, links[s], NT, preferred_element_type=F32)
            mapped[s] = jnp.concatenate([total, jnp.zeros((rows, half), F32)], axis=1)
            back[s] = lax.dot_general(
                (chirality * here[i])[:, :half].astype(BF16),
                links[s],
                NN,
                preferred_element_type=F32,
            )
    top = zero
    bottom = zero
    for s in range(box.count):
        behind = [box.behind(s, d) for d in range(4)]
        piece = []
        for d in range(4):
            start = d // 2 * lanes
            piece.append(zero if behind[d] is None else back[behind[d], :, start : start + lanes])
        gathered = jnp.where(low, piece[0], piece[1]) + jnp.where(low, piece[2], piece[3])
        gathered = chirality * gathered + mapped[s]
        here = field[s]
        value = 4.0 * here + gathered + pltpu.roll(gathered, half, 1)
        mapped[s] = value
        top = top + value * here
        bottom = bottom + value * value
    return jnp.sum(top, axis=1, keepdims=True) / jnp.sum(bottom, axis=1, keepdims=True)


def smooth(box, flips, field, links, own, outs, scratch, arrive=None):
    update, image, sends = outs
    back_a, back_b, map_a, map_b, second = scratch
    rows, lanes = field.shape[1:]
    half = lanes // 2
    low, chirality = lane_tools(rows, lanes)
    weight_a = local_products(box, field, links, own, back_a, map_a, low, chirality, arrive)
    for s in range(box.count):
        second[s] = field[s] - weight_a * map_a[s]
    weight_b = local_products(box, second, links, own, back_b, map_b, low, chirality)
    for s in range(box.count):
        update[s] = weight_a * field[s] + weight_b * second[s]
        image[s] = weight_a * map_a[s] + weight_b * map_b[s]
    for d in range(4):
        flip = flips[d]
        lower = box.rim(d, False)
        upper = box.rim(d, True)
        start = d // 2 * lanes
        for j in range(len(lower) // 4):
            block = []
            for k in (4 * j, 4 * j + 2):
                block.append(jnp.where(low, update[lower[k]], update[lower[k + 1]]))
            sends[d][flip, j] = jnp.concatenate(block, axis=0).astype(BF16)
            block = []
            for k in (4 * j, 4 * j + 2):
                pair = []
                for u in (upper[k], upper[k + 1]):
                    pair.append(
                        weight_a * back_a[u, :, start : start + lanes]
                        + weight_b * back_b[u, :, start : start + lanes]
                    )
                if d % 2 == 0:
                    joined = jnp.where(low, pair[0], pltpu.roll(pair[1], half, 1))
                else:
                    joined = jnp.where(low, pltpu.roll(pair[0], half, 1), pair[1])
                block.append(chirality * joined)
            sends[d][1 - flip, j] = jnp.concatenate(block, axis=0).astype(BF16)


def first_kernel(
    box, parts, flips, rhs_in, own_in, hop_in, *refs
):
    update, image, send0, send1, send2, send3, links, own = refs[:8]
    field, back_a, back_b, map_a, map_b, second, rhs, own_raw, hop, sems = refs[8:]
    each = box.count // parts
    copies = [pltpu.make_async_copy(rhs_in, rhs, sems.at[2 * parts])]
    for c in range(parts):
        run = pl.ds(c * each, each)
        copies.append(pltpu.make_async_copy(hop_in.at[:, run], hop.at[:, run], sems.at[2 * c]))
        copies.append(pltpu.make_async_copy(own_in.at[run], own_raw.at[run], sems.at[2 * c + 1]))
    for copy in copies:
        copy.start()
    copies[0].wait()
    for s in range(box.count):
        field[s] = twice(rhs[s])

    def arrive(g):
        if g * GROUP % each == 0:
            c = g * GROUP // each
            copies[2 * c + 1].wait()
            copies[2 * c + 2].wait()
        sites = range(GROUP * g, GROUP * g + GROUP)
        own[g] = jnp.concatenate([own_raw[s] for s in sites], axis=1)
        for s in sites:
            links[s] = jnp.concatenate([hop[d, s] for d in range(4)], axis=1)

    scratch = (back_a, back_b, map_a, map_b, second)
    smooth(box, flips, field, links, own, (update, image, (send0, send1, send2, send3)), scratch, arrive)


def second_kernel(box, flips, rhs, mapped, sums, links, own, update, image, send0, send1, send2, send3, field, *scratch):
    top, square = unpacked_sums(sums, 2, mapped.shape[1])
    alpha = top / square
    for s in range(box.count):
        field[s] = twice(rhs[s]) - alpha * mapped[s]
    smooth(box, flips, field, links, own, (update, image, (send0, send1, send2, send3)), scratch)


def joined_halo(box, flips, image, links, came, mapped, low):
    rows, lanes = image.shape[1:]
    half = lanes // 2

    places = [{s: k for k, s in enumerate(box.rim(d, True))} for d in range(4)]
    lows = [{s: k for k, s in enumerate(box.rim(d, False))} for d in range(4)]

    def read(d, which, k):
        slot = flips[d] if which == 0 else 1 - flips[d]
        tile = came[d][slot, k // 4].astype(F32)
        tile = tile[(k // 2 % 2) * rows : (k // 2 % 2 + 1) * rows]
        if which == 0 and k % 2 != d % 2:
            tile = pltpu.roll(tile, half, 1)
        return tile

    zero = jnp.zeros((rows, lanes), F32)
    for s in range(box.count):
        part = [read(d, 0, places[d][s]) if s in places[d] else None for d in range(4)]
        extra = zero
        if any(p is not None for p in part):
            part = [zero if p is None else p for p in part]
            spread = jnp.concatenate(
                [jnp.where(low, part[0], part[1]), jnp.where(low, part[2], part[3])], axis=1
            ).astype(BF16)
            total = lax.dot_general(spread, links[s], NT, preferred_element_type=F32)
            extra = jnp.concatenate([total, jnp.zeros((rows, half), F32)], axis=1)
        for d in range(4):
            if s in lows[d]:
                k = lows[d][s]
                tile = read(d, 1, k)
                extra = extra + (jnp.where(low, tile, 0.0) if k % 2 == 0 else jnp.where(low, 0.0, tile))
        mapped[s] = image[s] + extra + pltpu.roll(extra, half, 1)


def sum_places(rows, lanes):
    row = lax.broadcasted_iota(jnp.int32, (rows, lanes), 0)
    lane = lax.broadcasted_iota(jnp.int32, (rows, lanes), 1)
    return lane - row


def packed_sums(values, out):
    rows, lanes = values[0].shape
    places = sum_places(rows, lanes)
    spread = jnp.zeros((rows, lanes), F32)
    for k, value in enumerate(values):
        spread = jnp.where(places == k * rows, jnp.sum(value, axis=1, keepdims=True), spread)
    out[...] = jnp.broadcast_to(jnp.sum(spread, axis=0, keepdims=True), out.shape)


def unpacked_sums(sums, count, rows):
    lanes = sums.shape[1]
    total = jnp.broadcast_to(jnp.sum(sums[...], axis=0, keepdims=True), (rows, lanes))
    places = sum_places(rows, lanes)
    return [
        jnp.sum(jnp.where(places == k * rows, total, 0.0), axis=1, keepdims=True) for k in range(count)
    ]


def third_kernel(box, flips, rhs, image, links, came3, came2, came1, came0, mapped, sums):
    rows, lanes = image.shape[1:]
    low, _ = lane_tools(rows, lanes)
    joined_halo(box, flips, image, links, (came0, came1, came2, came3), mapped, low)
    zero = jnp.zeros((rows, lanes), F32)
    top = zero
    bottom = zero
    for s in range(box.count):
        value = mapped[s]
        top = top + value * twice(rhs[s])
        bottom = bottom + value * value
    packed_sums((top, bottom), sums)


def fourth_kernel(box, flips, rhs, first, before, image, links, came3, came2, came1, came0, mapped, sums):
    rows, lanes = image.shape[1:]
    low, _ = lane_tools(rows, lanes)
    joined_halo(box, flips, image, links, (came0, came1, came2, came3), mapped, low)
    top, square = unpacked_sums(before, 2, rows)
    alpha = top / square
    total = [jnp.zeros((rows, lanes), F32) for _ in range(4)]
    for s in range(box.count):
        old = first[s]
        value = mapped[s]
        remain = twice(rhs[s]) - alpha * old
        for k, product in enumerate((old * value, value * value, value * remain, old * remain)):
            total[k] = total[k] + product
    packed_sums(total, sums)


def last_kernel(box, rhs, update_a, map_a, update_b, map_b, sums_a, sums_b, solution_out, residual_out):
    rows, lanes = update_a.shape[1:]
    half = lanes // 2
    top, square = unpacked_sums(sums_a, 2, rows)
    alpha = top / square
    cross, norm, raw, old = unpacked_sums(sums_b, 4, rows)
    beta = cross / square
    step = (raw - beta * old) / (norm - 2.0 * beta * cross + beta * beta * square)
    for s in range(box.count):
        old = update_a[s][:, :half]
        solution_out[s] = alpha * old + step * (update_b[s][:, :half] - beta * old)
        old = map_a[s][:, :half]
        residual_out[s] = rhs[s] - alpha * old - step * (map_b[s][:, :half] - beta * old)


def call(body, outs, scratch, ins, flips=None, space=pltpu.VMEM):
    vmem = pl.BlockSpec(memory_space=pltpu.VMEM)
    specs = [pl.BlockSpec(memory_space=space)] * len(ins)
    if flips is not None:
        specs.insert(0, pl.BlockSpec(memory_space=pltpu.SMEM))
        ins = (flips, *ins)
    return pl.pallas_call(
        body,
        out_shape=outs,
        in_specs=specs,
        out_specs=[vmem] * len(outs),
        scratch_shapes=scratch,
        compiler_params=pltpu.CompilerParams(vmem_limit_bytes=VMEM_BYTES),
    )(*ins)


def plan(direction):
    axis = AXES[direction]
    size = lax.axis_size(axis)
    step = min(8, max(2, lax.axis_size("gx") // 8)) if direction == 0 else 1
    if 2 * step % size == 0:
        return axis, size, step, "both"
    if step == 1 and size % 2 == 0:
        return axis, size, step, "pairs"
    return axis, size, step, "shift"


def message_tiles(box):
    tiles = [len(box.rim(d, True)) // 4 for d in range(4)]
    longest = 2 * max(tiles[:2])
    return tiles[:2] + [longest // 2 + 1, longest + 1]


def exchange(sends):
    came = [None] * 4
    for d in reversed(range(4)):
        axis, size, step, kind = plan(d)
        ring = range(size)
        if kind == "both":
            came[d] = lax.ppermute(sends[d], axis, [(i, (i + step) % size) for i in ring])
        elif kind == "pairs":
            even = lax.ppermute(sends[d][0], axis, [(i, i ^ 1) for i in ring])
            odd = lax.ppermute(sends[d][1], axis, [(i, (i + 1 if i % 2 else i - 1) % size) for i in ring])
            came[d] = jnp.stack([even, odd])
        else:
            field = lax.ppermute(sends[d][0], axis, [(i, (i - step) % size) for i in ring])
            back = lax.ppermute(sends[d][1], axis, [(i, (i + step) % size) for i in ring])
            came[d] = jnp.stack([field, back])
    return came


def device_count():
    return lax.axis_size("gx") * lax.axis_size("gz") * lax.axis_size("ta")


def sum_rows():
    return device_count() if device_count() <= 64 else 1


def mesh_sum(value):
    if sum_rows() > 1:
        return lax.all_to_all(value, ("gx", "gz", "ta"), 0, 0, tiled=True)
    for axis in ("gx", "gz", "ta"):
        size = lax.axis_size(axis)
        if size & (size - 1):
            value = lax.psum(value, axis)
            continue
        hop = 1
        while hop < size:
            value = value + lax.ppermute(value, axis, [(i, i ^ hop) for i in range(size)])
            hop *= 2
    return value


def on_device(rhs, self_coupling, hopping):
    extents = rhs.shape[1:5]
    rows, channels = rhs.shape[5:]
    lanes = 2 * channels
    box = Box(extents)
    count = box.count
    source = rhs.reshape(count, rows, channels)
    own = self_coupling.reshape(count, channels, channels)
    hop = hopping.reshape(4, count, channels, channels)

    flips_out = []
    flips_in = []
    for d in range(4):
        axis, _, _, kind = plan(d)
        if kind == "pairs":
            odd = lax.axis_index(axis) % 2
            flips_out.append(1 - odd)
            flips_in.append(odd)
        else:
            flips_out.append(jnp.int32(0))
            flips_in.append(jnp.int32(0))
    flips_out = jnp.stack(flips_out).astype(jnp.int32)
    flips_in = jnp.stack(flips_in).astype(jnp.int32)

    full = jax.ShapeDtypeStruct((count, rows, lanes), F32)
    small = jax.ShapeDtypeStruct((sum_rows(), lanes), F32)
    narrow = jax.ShapeDtypeStruct((count, rows, channels), F32)
    links_shape = jax.ShapeDtypeStruct((count, channels, 4 * channels), BF16)
    own_shape = jax.ShapeDtypeStruct((count // GROUP, channels, GROUP * channels), BF16)
    parts = extents[0] * extents[1]
    raw = [
        pltpu.VMEM(source.shape, F32),
        pltpu.VMEM(own.shape, BF16),
        pltpu.VMEM(hop.shape, BF16),
        pltpu.SemaphoreType.DMA((2 * parts + 1,)),
    ]
    send_shapes = [
        jax.ShapeDtypeStruct((2, tiles, 2 * rows, lanes), BF16) for tiles in message_tiles(box)
    ]
    field_scratch = pltpu.VMEM((count, rows, lanes), F32)
    back_scratch = pltpu.VMEM((count, rows, 4 * channels), F32)
    scratch = [field_scratch, back_scratch, back_scratch, field_scratch, field_scratch, field_scratch]

    update_a, image_a, *sends, links, own = call(
        functools.partial(first_kernel, box, parts),
        [full, full, *send_shapes, links_shape, own_shape],
        scratch + raw,
        [pltpu.with_memory_space_constraint(a, pltpu.HBM) for a in (source, own, hop)],
        flips_out,
        pltpu.HBM,
    )
    came = exchange(sends)
    map_a, sums_a = call(
        functools.partial(third_kernel, box), [full, small], [], (source, image_a, links, *came[::-1]), flips_in
    )
    sums_a = mesh_sum(sums_a)
    update_b, image_b, *sends = call(
        functools.partial(second_kernel, box),
        [full, full, *send_shapes],
        scratch,
        (source, map_a, sums_a, links, own),
        flips_out,
    )
    came = exchange(sends)
    map_b, sums_b = call(
        functools.partial(fourth_kernel, box),
        [full, small],
        [],
        (source, map_a, sums_a, image_b, links, *came[::-1]),
        flips_in,
    )
    sums_b = mesh_sum(sums_b)
    found, left = call(
        functools.partial(last_kernel, box),
        [narrow, narrow],
        [],
        (source, update_a, map_a, update_b, map_b, sums_a, sums_b),
    )
    return found.reshape(rhs.shape), left.reshape(rhs.shape)


def solution(mesh):
    in_specs = (
        P("gx", None, None, "gz", "ta", None, None),
        P("gx", None, None, "gz", "ta", None, None),
        P(None, "gx", None, None, "gz", "ta", None, None),
    )
    out_specs = (
        P("gx", None, None, "gz", "ta", None, None),
        P("gx", None, None, "gz", "ta", None, None),
    )
    return jax.shard_map(
        on_device, mesh=mesh, in_specs=in_specs, out_specs=out_specs, check_vma=False
    )
```

```python
import functools

import jax
import jax.numpy as jnp
from jax import lax
from jax.experimental import pallas as pl
from jax.experimental.pallas import tpu as pltpu
from jax.sharding import PartitionSpec as P

F32 = jnp.float32
BF16 = jnp.bfloat16
NT = (((1,), (1,)), ((), ()))
NN = (((1,), (0,)), ((), ()))
VMEM_BYTES = 24 * 2**20
GROUP = 4
LAG = 2
AXES = ("gx", "gx", "gz", "ta")


class Box:
    def __init__(self, extents):
        self.extents = tuple(extents)
        self.strides = []
        count = 1
        for extent in reversed(self.extents):
            self.strides.insert(0, count)
            count *= extent
        self.count = count

    def coord(self, site, direction):
        return site // self.strides[direction] % self.extents[direction]

    def ahead(self, site, direction):
        last = self.extents[direction] - 1
        return None if self.coord(site, direction) == last else site + self.strides[direction]

    def behind(self, site, direction):
        return None if self.coord(site, direction) == 0 else site - self.strides[direction]

    def rim(self, direction, upper):
        wanted = self.extents[direction] - 1 if upper else 0
        return [s for s in range(self.count) if self.coord(s, direction) == wanted]


class Tiles:
    def __init__(self, blocks, first):
        self.first = first
        self.tiles = [blocks[k : k + 4] for k in range(0, len(blocks), 4)]
        self.sites = [list(dict.fromkeys(s for s, _ in tile)) for tile in self.tiles]
        self.starts = []
        self.place = {}
        self.runs = 0
        for tile, sites in zip(self.tiles, self.sites):
            self.starts.append(self.runs)
            for slot, block in enumerate(tile):
                self.place[block] = (self.runs + sites.index(block[0]), slot)
            self.runs += len(sites)


def split_links(box):
    blocks = [(s, d) for s in range(box.count) for d in range(4)]
    inner = Tiles([b for b in blocks if box.ahead(*b) is not None], 0)
    outer = Tiles([b for b in blocks if box.ahead(*b) is None], len(inner.tiles))
    return inner, outer


def slotted(contents, low, zero):
    halves = []
    for left, right in (contents[:2], contents[2:]):
        if left is None and right is None:
            halves.append(zero)
        else:
            halves.append(jnp.where(low, zero if left is None else left, zero if right is None else right))
    return jnp.concatenate(halves, axis=1)


def ahead_products(tiles, k, value, links, low, zero):
    rows = zero.shape[0]
    stack = []
    for s in tiles.sites[k]:
        contents = [value(s, d, slot) if t == s else None for slot, (t, d) in enumerate(tiles.tiles[k])]
        contents += [None] * (4 - len(contents))
        stack.append(slotted(contents, low, zero))
    spread = jnp.concatenate(stack, axis=0).astype(BF16)
    total = lax.dot_general(spread, links[tiles.first + k], NT, preferred_element_type=F32)
    return {s: total[i * rows : (i + 1) * rows] for i, s in enumerate(tiles.sites[k])}


def back_products(tiles, k, field, links, back, chirality):
    rows, lanes = field.shape[1:]
    stack = jnp.concatenate([chirality * field[s] for s in tiles.sites[k]], axis=0)
    product = lax.dot_general(
        stack[:, : lanes // 2].astype(BF16), links[tiles.first + k], NN, preferred_element_type=F32
    )
    for i in range(len(tiles.sites[k])):
        back[tiles.starts[k] + i] = product[i * rows : (i + 1) * rows]


def back_value(tiles, block, back, lanes):
    run, slot = tiles.place[block]
    return back[run, :, slot // 2 * lanes : (slot // 2 + 1) * lanes], slot % 2


def lane_tools(rows, lanes):
    lane = lax.broadcasted_iota(jnp.int32, (rows, lanes), 1)
    low = lane < lanes // 2
    chirality = jnp.where(lane % (lanes // 2) < lanes // 4, 1.0, -1.0).astype(F32)
    return low, chirality


def twice(value):
    return jnp.concatenate([value, value], axis=1)


def own_products(group, here, own, low):
    rows, lanes = here[0].shape
    zero = jnp.zeros((rows, lanes), F32)
    left = [jnp.where(low, here[0], 0.0), jnp.where(low, 0.0, here[1]), zero, zero]
    right = [zero, zero, jnp.where(low, here[2], 0.0), jnp.where(low, 0.0, here[3])]
    blocks = jnp.concatenate(
        [jnp.concatenate(left, axis=0), jnp.concatenate(right, axis=0)], axis=1
    ).astype(BF16)
    return lax.dot_general(blocks, own[group], NT, preferred_element_type=F32)


def local_products(box, tiles, field, links, own, back, mapped, low, chirality, prepare=None):
    rows, lanes = field.shape[1:]
    half = lanes // 2
    zero = jnp.zeros((rows, lanes), F32)
    top = [zero]
    bottom = [zero]
    parts = {}

    def value(s, d, _):
        return field[box.ahead(s, d)]

    def diagonal(g):
        if prepare is not None:
            prepare(group=g)
        sites = range(GROUP * g, GROUP * g + GROUP)
        total = own_products(g, [field[s] for s in sites], own, low)
        for i, s in enumerate(sites):
            parts[s] = total[i * rows : (i + 1) * rows]

    def gather(s):
        sums = [None, None]
        for d in range(4):
            b = box.behind(s, d)
            if b is not None:
                piece, side = back_value(tiles, (b, d), back, lanes)
                sums[side] = piece if sums[side] is None else sums[side] + piece
        gathered = mapped[s]
        if sums[0] is not None or sums[1] is not None:
            sums = [zero if x is None else x for x in sums]
            gathered = chirality * jnp.where(low, sums[0], sums[1]) + gathered
        here = field[s]
        result = 4.0 * here + gathered + pltpu.roll(gathered, half, 1)
        mapped[s] = result
        top[0] = top[0] + result * here
        bottom[0] = bottom[0] + result * result

    last = {}
    for k, sites in enumerate(tiles.sites):
        for s in sites:
            last[s] = k
    ready = 0
    done = 0
    for k in range(len(tiles.tiles) + LAG):
        if k < len(tiles.tiles):
            for s in tiles.sites[k]:
                while ready * GROUP <= s:
                    diagonal(ready)
                    ready += 1
            if prepare is not None:
                prepare(tile=k)
            for s, part in ahead_products(tiles, k, value, links, low, zero).items():
                parts[s] = parts[s] + part
            back_products(tiles, k, field, links, back, chirality)
            for s in tiles.sites[k]:
                if last[s] == k:
                    mapped[s] = jnp.concatenate([parts.pop(s), jnp.zeros((rows, half), F32)], axis=1)
        if k >= LAG:
            while done < box.count and last.get(done, -1) <= k - LAG and done // GROUP < ready:
                if done in parts:
                    mapped[done] = jnp.concatenate([parts.pop(done), jnp.zeros((rows, half), F32)], axis=1)
                gather(done)
                done += 1
    while ready * GROUP < box.count:
        diagonal(ready)
        ready += 1
    while done < box.count:
        if done in parts:
            mapped[done] = jnp.concatenate([parts.pop(done), jnp.zeros((rows, half), F32)], axis=1)
        gather(done)
        done += 1
    return jnp.sum(top[0], axis=1, keepdims=True) / jnp.sum(bottom[0], axis=1, keepdims=True)


def smooth(box, flips, field, links, own, outs, scratch, prepare=None):
    update, image, sends = outs
    back, map_a, map_b, second = scratch
    rows, lanes = field.shape[1:]
    half = lanes // 2
    low, chirality = lane_tools(rows, lanes)
    inner, outer = split_links(box)
    weight_a = local_products(box, inner, field, links, own, back, map_a, low, chirality, prepare)
    for s in range(box.count):
        second[s] = field[s] - weight_a * map_a[s]
    weight_b = local_products(box, inner, second, links, own, back, map_b, low, chirality)
    for s in range(box.count):
        update[s] = weight_a * field[s] + weight_b * second[s]
    for k in range(len(outer.tiles)):
        back_products(outer, k, update, links, back, chirality)
    for s in range(box.count):
        image[s] = weight_a * map_a[s] + weight_b * map_b[s]

    def aligned(s, d, side):
        piece, found = back_value(outer, (s, d), back, lanes)
        return piece if found == side else pltpu.roll(piece, half, 1)

    for d in range(4):
        flip = flips[d]
        lower = box.rim(d, False)
        upper = box.rim(d, True)
        for j in range(len(lower) // 4):
            block = []
            for k in (4 * j, 4 * j + 2):
                block.append(jnp.where(low, update[lower[k]], update[lower[k + 1]]))
            sends[d][flip, j] = jnp.concatenate(block, axis=0).astype(BF16)
            block = []
            for k in (4 * j, 4 * j + 2):
                joined = jnp.where(low, aligned(upper[k], d, 0), aligned(upper[k + 1], d, 1))
                block.append(chirality * joined)
            sends[d][1 - flip, j] = jnp.concatenate(block, axis=0).astype(BF16)


def first_kernel(
    box, parts, flips, rhs_in, own_in, hop_in, *refs
):
    update, image, send0, send1, send2, send3, links, own = refs[:8]
    field, back, map_a, map_b, second, rhs, own_raw, hop, sems = refs[8:]
    each = box.count // parts
    copies = [pltpu.make_async_copy(rhs_in, rhs, sems.at[2 * parts])]
    for c in range(parts):
        run = pl.ds(c * each, each)
        copies.append(pltpu.make_async_copy(hop_in.at[:, run], hop.at[:, run], sems.at[2 * c]))
        copies.append(pltpu.make_async_copy(own_in.at[run], own_raw.at[run], sems.at[2 * c + 1]))
    for copy in copies:
        copy.start()
    copies[0].wait()
    for s in range(box.count):
        field[s] = twice(rhs[s])
    inner, outer = split_links(box)
    blank = jnp.zeros(hop.shape[2:], BF16)
    arrived = [0]
    packed = [0]

    def await_site(s):
        while arrived[0] * each <= s:
            c = arrived[0]
            copies[2 * c + 1].wait()
            copies[2 * c + 2].wait()
            arrived[0] += 1

    def pack(tiles, k):
        matrices = [hop[d, s] for s, d in tiles.tiles[k]]
        matrices += [blank] * (4 - len(matrices))
        links[tiles.first + k] = jnp.concatenate(matrices, axis=1)

    def prepare(group=None, tile=None):
        if group is not None:
            sites = range(GROUP * group, GROUP * group + GROUP)
            await_site(sites[-1])
            own[group] = jnp.concatenate([own_raw[s] for s in sites], axis=1)
        if tile is not None:
            await_site(inner.sites[tile][-1])
            pack(inner, tile)
            final = tile == len(inner.tiles) - 1
            if final:
                await_site(box.count - 1)
            while packed[0] < len(outer.tiles) and (final or outer.sites[packed[0]][-1] < arrived[0] * each):
                pack(outer, packed[0])
                packed[0] += 1
                if not final and packed[0] * len(inner.tiles) > (tile + 1) * len(outer.tiles):
                    break

    scratch = (back, map_a, map_b, second)
    smooth(box, flips, field, links, own, (update, image, (send0, send1, send2, send3)), scratch, prepare)


def second_kernel(box, flips, rhs, mapped, sums, links, own, update, image, send0, send1, send2, send3, field, *scratch):
    top, square = unpacked_sums(sums, 2, mapped.shape[1])
    alpha = top / square
    for s in range(box.count):
        field[s] = twice(rhs[s]) - alpha * mapped[s]
    smooth(box, flips, field, links, own, (update, image, (send0, send1, send2, send3)), scratch)


def joined_halo(box, flips, image, links, came, mapped, low):
    rows, lanes = image.shape[1:]
    half = lanes // 2

    places = [{s: k for k, s in enumerate(box.rim(d, True))} for d in range(4)]
    lows = [{s: k for k, s in enumerate(box.rim(d, False))} for d in range(4)]

    def read(d, which, k):
        slot = flips[d] if which == 0 else 1 - flips[d]
        tile = came[d][slot, k // 4].astype(F32)
        return tile[(k // 2 % 2) * rows : (k // 2 % 2 + 1) * rows]

    zero = jnp.zeros((rows, lanes), F32)
    _, outer = split_links(box)

    def value(s, d, slot):
        k = places[d][s]
        tile = read(d, 0, k)
        return tile if k % 2 == slot % 2 else pltpu.roll(tile, half, 1)

    parts = {}
    last = {}
    for k, sites in enumerate(outer.sites):
        for s in sites:
            last[s] = k

    def finish(s):
        extra = zero
        if s in parts:
            extra = jnp.concatenate([parts.pop(s), jnp.zeros((rows, half), F32)], axis=1)
        for d in range(4):
            if s in lows[d]:
                k = lows[d][s]
                tile = read(d, 1, k)
                extra = extra + (jnp.where(low, tile, 0.0) if k % 2 == 0 else jnp.where(low, 0.0, tile))
        mapped[s] = image[s] + extra + pltpu.roll(extra, half, 1)

    done = 0
    for k in range(len(outer.tiles)):
        for s, part in ahead_products(outer, k, value, links, low, zero).items():
            parts[s] = parts[s] + part if s in parts else part
        while done < box.count and last.get(done, -1) <= k - LAG:
            finish(done)
            done += 1
    for s in range(done, box.count):
        finish(s)


def sum_places(rows, lanes):
    row = lax.broadcasted_iota(jnp.int32, (rows, lanes), 0)
    lane = lax.broadcasted_iota(jnp.int32, (rows, lanes), 1)
    return lane - row


def packed_sums(values, out):
    rows, lanes = values[0].shape
    places = sum_places(rows, lanes)
    spread = jnp.zeros((rows, lanes), F32)
    for k, value in enumerate(values):
        spread = jnp.where(places == k * rows, jnp.sum(value, axis=1, keepdims=True), spread)
    out[...] = jnp.broadcast_to(jnp.sum(spread, axis=0, keepdims=True), out.shape)


def unpacked_sums(sums, count, rows):
    lanes = sums.shape[1]
    total = jnp.broadcast_to(jnp.sum(sums[...], axis=0, keepdims=True), (rows, lanes))
    places = sum_places(rows, lanes)
    return [
        jnp.sum(jnp.where(places == k * rows, total, 0.0), axis=1, keepdims=True) for k in range(count)
    ]


def third_kernel(box, flips, rhs, image, links, came3, came2, came1, came0, mapped, sums):
    rows, lanes = image.shape[1:]
    low, _ = lane_tools(rows, lanes)
    joined_halo(box, flips, image, links, (came0, came1, came2, came3), mapped, low)
    zero = jnp.zeros((rows, lanes), F32)
    top = zero
    bottom = zero
    for s in range(box.count):
        value = mapped[s]
        top = top + value * twice(rhs[s])
        bottom = bottom + value * value
    packed_sums((top, bottom), sums)


def fourth_kernel(box, flips, rhs, first, before, image, links, came3, came2, came1, came0, mapped, sums):
    rows, lanes = image.shape[1:]
    low, _ = lane_tools(rows, lanes)
    joined_halo(box, flips, image, links, (came0, came1, came2, came3), mapped, low)
    top, square = unpacked_sums(before, 2, rows)
    alpha = top / square
    total = [jnp.zeros((rows, lanes), F32) for _ in range(4)]
    for s in range(box.count):
        old = first[s]
        value = mapped[s]
        remain = twice(rhs[s]) - alpha * old
        for k, product in enumerate((old * value, value * value, value * remain, old * remain)):
            total[k] = total[k] + product
    packed_sums(total, sums)


def last_kernel(box, rhs, update_a, map_a, update_b, map_b, sums_a, sums_b, solution_out, residual_out):
    rows, lanes = update_a.shape[1:]
    half = lanes // 2
    top, square = unpacked_sums(sums_a, 2, rows)
    alpha = top / square
    cross, norm, raw, old = unpacked_sums(sums_b, 4, rows)
    beta = cross / square
    step = (raw - beta * old) / (norm - 2.0 * beta * cross + beta * beta * square)
    for s in range(box.count):
        old = update_a[s][:, :half]
        solution_out[s] = alpha * old + step * (update_b[s][:, :half] - beta * old)
        old = map_a[s][:, :half]
        residual_out[s] = rhs[s] - alpha * old - step * (map_b[s][:, :half] - beta * old)


def call(body, outs, scratch, ins, flips=None, space=pltpu.VMEM):
    vmem = pl.BlockSpec(memory_space=pltpu.VMEM)
    specs = [pl.BlockSpec(memory_space=space)] * len(ins)
    if flips is not None:
        specs.insert(0, pl.BlockSpec(memory_space=pltpu.SMEM))
        ins = (flips, *ins)
    return pl.pallas_call(
        body,
        out_shape=outs,
        in_specs=specs,
        out_specs=[vmem] * len(outs),
        scratch_shapes=scratch,
        compiler_params=pltpu.CompilerParams(vmem_limit_bytes=VMEM_BYTES),
    )(*ins)


def plan(direction):
    axis = AXES[direction]
    size = lax.axis_size(axis)
    step = min(8, max(2, lax.axis_size("gx") // 8)) if direction == 0 else 1
    if 2 * step % size == 0:
        return axis, size, step, "both"
    if step == 1 and size % 2 == 0:
        return axis, size, step, "pairs"
    return axis, size, step, "shift"


def message_tiles(box):
    tiles = [len(box.rim(d, True)) // 4 for d in range(4)]
    longest = 2 * max(tiles[:2])
    return tiles[:2] + [longest // 2 + 1, longest + 1]


def exchange(sends):
    came = [None] * 4
    for d in reversed(range(4)):
        axis, size, step, kind = plan(d)
        ring = range(size)
        if kind == "both":
            came[d] = lax.ppermute(sends[d], axis, [(i, (i + step) % size) for i in ring])
        elif kind == "pairs":
            even = lax.ppermute(sends[d][0], axis, [(i, i ^ 1) for i in ring])
            odd = lax.ppermute(sends[d][1], axis, [(i, (i + 1 if i % 2 else i - 1) % size) for i in ring])
            came[d] = jnp.stack([even, odd])
        else:
            field = lax.ppermute(sends[d][0], axis, [(i, (i - step) % size) for i in ring])
            back = lax.ppermute(sends[d][1], axis, [(i, (i + step) % size) for i in ring])
            came[d] = jnp.stack([field, back])
    return came


def device_count():
    return lax.axis_size("gx") * lax.axis_size("gz") * lax.axis_size("ta")


def sum_rows():
    return device_count() if device_count() <= 64 else 1


def mesh_sum(value):
    if sum_rows() > 1:
        return lax.all_to_all(value, ("gx", "gz", "ta"), 0, 0, tiled=True)
    for axis in ("gx", "gz", "ta"):
        size = lax.axis_size(axis)
        if size & (size - 1):
            value = lax.psum(value, axis)
            continue
        hop = 1
        while hop < size:
            value = value + lax.ppermute(value, axis, [(i, i ^ hop) for i in range(size)])
            hop *= 2
    return value


def on_device(rhs, self_coupling, hopping):
    extents = rhs.shape[1:5]
    rows, channels = rhs.shape[5:]
    lanes = 2 * channels
    box = Box(extents)
    count = box.count
    source = rhs.reshape(count, rows, channels)
    own = self_coupling.reshape(count, channels, channels)
    hop = hopping.reshape(4, count, channels, channels)

    flips_out = []
    flips_in = []
    for d in range(4):
        axis, _, _, kind = plan(d)
        if kind == "pairs":
            odd = lax.axis_index(axis) % 2
            flips_out.append(1 - odd)
            flips_in.append(odd)
        else:
            flips_out.append(jnp.int32(0))
            flips_in.append(jnp.int32(0))
    flips_out = jnp.stack(flips_out).astype(jnp.int32)
    flips_in = jnp.stack(flips_in).astype(jnp.int32)

    full = jax.ShapeDtypeStruct((count, rows, lanes), F32)
    small = jax.ShapeDtypeStruct((sum_rows(), lanes), F32)
    narrow = jax.ShapeDtypeStruct((count, rows, channels), F32)
    inner, outer = split_links(box)
    link_tiles = len(inner.tiles) + len(outer.tiles)
    links_shape = jax.ShapeDtypeStruct((link_tiles, channels, 4 * channels), BF16)
    own_shape = jax.ShapeDtypeStruct((count // GROUP, channels, GROUP * channels), BF16)
    parts = extents[0] * extents[1]
    raw = [
        pltpu.VMEM(source.shape, F32),
        pltpu.VMEM(own.shape, BF16),
        pltpu.VMEM(hop.shape, BF16),
        pltpu.SemaphoreType.DMA((2 * parts + 1,)),
    ]
    send_shapes = [
        jax.ShapeDtypeStruct((2, tiles, 2 * rows, lanes), BF16) for tiles in message_tiles(box)
    ]
    field_scratch = pltpu.VMEM((count, rows, lanes), F32)
    back_scratch = pltpu.VMEM((max(inner.runs, outer.runs), rows, 4 * channels), F32)
    scratch = [field_scratch, back_scratch, field_scratch, field_scratch, field_scratch]

    update_a, image_a, *sends, links, own = call(
        functools.partial(first_kernel, box, parts),
        [full, full, *send_shapes, links_shape, own_shape],
        scratch + raw,
        [pltpu.with_memory_space_constraint(a, pltpu.HBM) for a in (source, own, hop)],
        flips_out,
        pltpu.HBM,
    )
    came = exchange(sends)
    map_a, sums_a = call(
        functools.partial(third_kernel, box), [full, small], [], (source, image_a, links, *came[::-1]), flips_in
    )
    sums_a = mesh_sum(sums_a)
    update_b, image_b, *sends = call(
        functools.partial(second_kernel, box),
        [full, full, *send_shapes],
        scratch,
        (source, map_a, sums_a, links, own),
        flips_out,
    )
    came = exchange(sends)
    map_b, sums_b = call(
        functools.partial(fourth_kernel, box),
        [full, small],
        [],
        (source, map_a, sums_a, image_b, links, *came[::-1]),
        flips_in,
    )
    sums_b = mesh_sum(sums_b)
    found, left = call(
        functools.partial(last_kernel, box),
        [narrow, narrow],
        [],
        (source, update_a, map_a, update_b, map_b, sums_a, sums_b),
    )
    return found.reshape(rhs.shape), left.reshape(rhs.shape)


def solution(mesh):
    in_specs = (
        P("gx", None, None, "gz", "ta", None, None),
        P("gx", None, None, "gz", "ta", None, None),
        P(None, "gx", None, None, "gz", "ta", None, None),
    )
    out_specs = (
        P("gx", None, None, "gz", "ta", None, None),
        P("gx", None, None, "gz", "ta", None, None),
    )
    return jax.shard_map(
        on_device, mesh=mesh, in_specs=in_specs, out_specs=out_specs, check_vma=False
    )
```

```python
import functools

import jax
import jax.numpy as jnp
from jax import lax
from jax.experimental import pallas as pl
from jax.experimental.pallas import tpu as pltpu
from jax.sharding import PartitionSpec as P

F32 = jnp.float32
BF16 = jnp.bfloat16
NT = (((1,), (1,)), ((), ()))
NN = (((1,), (0,)), ((), ()))
VMEM_BYTES = 24 * 2**20
GROUP = 4
LAG = 2
AXES = ("gx", "gx", "gz", "ta")


class Box:
    def __init__(self, extents):
        self.extents = tuple(extents)
        self.strides = []
        count = 1
        for extent in reversed(self.extents):
            self.strides.insert(0, count)
            count *= extent
        self.count = count

    def coord(self, site, direction):
        return site // self.strides[direction] % self.extents[direction]

    def ahead(self, site, direction):
        last = self.extents[direction] - 1
        return None if self.coord(site, direction) == last else site + self.strides[direction]

    def behind(self, site, direction):
        return None if self.coord(site, direction) == 0 else site - self.strides[direction]

    def rim(self, direction, upper):
        wanted = self.extents[direction] - 1 if upper else 0
        return [s for s in range(self.count) if self.coord(s, direction) == wanted]


class Tiles:
    def __init__(self, blocks, first):
        self.first = first
        self.tiles = [blocks[k : k + 4] for k in range(0, len(blocks), 4)]
        self.sites = [list(dict.fromkeys(s for s, _ in tile)) for tile in self.tiles]
        self.starts = []
        self.place = {}
        self.runs = 0
        for tile, sites in zip(self.tiles, self.sites):
            self.starts.append(self.runs)
            for slot, block in enumerate(tile):
                self.place[block] = (self.runs + sites.index(block[0]), slot)
            self.runs += len(sites)


def split_links(box):
    blocks = [(s, d) for s in range(box.count) for d in range(4)]
    inner = Tiles([b for b in blocks if box.ahead(*b) is not None], 0)
    outer = Tiles([b for b in blocks if box.ahead(*b) is None], len(inner.tiles))
    return inner, outer


def slotted(contents, low, zero):
    halves = []
    for left, right in (contents[:2], contents[2:]):
        if left is None and right is None:
            halves.append(zero)
        else:
            halves.append(jnp.where(low, zero if left is None else left, zero if right is None else right))
    return jnp.concatenate(halves, axis=1)


def ahead_products(tiles, k, value, links, low, zero):
    rows = zero.shape[0]
    stack = []
    for s in tiles.sites[k]:
        contents = [value(s, d, slot) if t == s else None for slot, (t, d) in enumerate(tiles.tiles[k])]
        contents += [None] * (4 - len(contents))
        stack.append(slotted(contents, low, zero))
    spread = jnp.concatenate(stack, axis=0).astype(BF16)
    total = lax.dot_general(spread, links[tiles.first + k], NT, preferred_element_type=F32)
    return {s: total[i * rows : (i + 1) * rows] for i, s in enumerate(tiles.sites[k])}


def back_products(tiles, k, field, links, back, chirality):
    rows, lanes = field.shape[1:]
    stack = jnp.concatenate([chirality * field[s] for s in tiles.sites[k]], axis=0)
    product = lax.dot_general(
        stack[:, : lanes // 2].astype(BF16), links[tiles.first + k], NN, preferred_element_type=F32
    )
    for i in range(len(tiles.sites[k])):
        back[tiles.starts[k] + i] = product[i * rows : (i + 1) * rows]


def back_value(tiles, block, back, lanes):
    run, slot = tiles.place[block]
    return back[run, :, slot // 2 * lanes : (slot // 2 + 1) * lanes], slot % 2


def lane_tools(rows, lanes):
    lane = lax.broadcasted_iota(jnp.int32, (rows, lanes), 1)
    low = lane < lanes // 2
    chirality = jnp.where(lane % (lanes // 2) < lanes // 4, 1.0, -1.0).astype(F32)
    return low, chirality


def twice(value):
    return jnp.concatenate([value, value], axis=1)


def own_products(group, here, own, low):
    rows, lanes = here[0].shape
    zero = jnp.zeros((rows, lanes), F32)
    left = [jnp.where(low, here[0], 0.0), jnp.where(low, 0.0, here[1]), zero, zero]
    right = [zero, zero, jnp.where(low, here[2], 0.0), jnp.where(low, 0.0, here[3])]
    blocks = jnp.concatenate(
        [jnp.concatenate(left, axis=0), jnp.concatenate(right, axis=0)], axis=1
    ).astype(BF16)
    return lax.dot_general(blocks, own[group], NT, preferred_element_type=F32)


def local_products(box, tiles, field, links, own, back, mapped, low, chirality, prepare=None):
    rows, lanes = field.shape[1:]
    half = lanes // 2
    zero = jnp.zeros((rows, lanes), F32)
    top = [zero]
    bottom = [zero]
    parts = {}

    def value(s, d, _):
        return field[box.ahead(s, d)]

    def diagonal(g):
        if prepare is not None:
            prepare(group=g)
        sites = range(GROUP * g, GROUP * g + GROUP)
        total = own_products(g, [field[s] for s in sites], own, low)
        for i, s in enumerate(sites):
            parts[s] = total[i * rows : (i + 1) * rows]

    def gather(s):
        sums = [None, None]
        for d in range(4):
            b = box.behind(s, d)
            if b is not None:
                piece, side = back_value(tiles, (b, d), back, lanes)
                sums[side] = piece if sums[side] is None else sums[side] + piece
        gathered = mapped[s]
        if sums[0] is not None or sums[1] is not None:
            sums = [zero if x is None else x for x in sums]
            gathered = chirality * jnp.where(low, sums[0], sums[1]) + gathered
        here = field[s]
        result = 4.0 * here + gathered + pltpu.roll(gathered, half, 1)
        mapped[s] = result
        top[0] = top[0] + result * here
        bottom[0] = bottom[0] + result * result

    last = {}
    for k, sites in enumerate(tiles.sites):
        for s in sites:
            last[s] = k
    ready = 0
    done = 0
    for k in range(len(tiles.tiles) + LAG):
        if k < len(tiles.tiles):
            for s in tiles.sites[k]:
                while ready * GROUP <= s:
                    diagonal(ready)
                    ready += 1
            if prepare is not None:
                prepare(tile=k)
            for s, part in ahead_products(tiles, k, value, links, low, zero).items():
                parts[s] = parts[s] + part
            back_products(tiles, k, field, links, back, chirality)
            for s in tiles.sites[k]:
                if last[s] == k:
                    mapped[s] = jnp.concatenate([parts.pop(s), jnp.zeros((rows, half), F32)], axis=1)
        if k >= LAG:
            while done < box.count and last.get(done, -1) <= k - LAG and done // GROUP < ready:
                if done in parts:
                    mapped[done] = jnp.concatenate([parts.pop(done), jnp.zeros((rows, half), F32)], axis=1)
                gather(done)
                done += 1
    while ready * GROUP < box.count:
        diagonal(ready)
        ready += 1
    while done < box.count:
        if done in parts:
            mapped[done] = jnp.concatenate([parts.pop(done), jnp.zeros((rows, half), F32)], axis=1)
        gather(done)
        done += 1
    return jnp.sum(top[0], axis=1, keepdims=True) / jnp.sum(bottom[0], axis=1, keepdims=True)


def came_slots(kinds):
    return [lax.axis_index(AXES[d]) % 2 if kinds[d] == "pairs" else 0 for d in range(4)]


def sent_slots(kinds):
    return [1 - slot if kind == "pairs" else 0 for kind, slot in zip(kinds, came_slots(kinds))]


def smooth(box, flips, field, links, own, outs, scratch, prepare=None):
    update, image, sends = outs
    back, map_a, map_b, second = scratch
    rows, lanes = field.shape[1:]
    half = lanes // 2
    low, chirality = lane_tools(rows, lanes)
    inner, outer = split_links(box)
    weight_a = local_products(box, inner, field, links, own, back, map_a, low, chirality, prepare)
    for s in range(box.count):
        second[s] = field[s] - weight_a * map_a[s]
    weight_b = local_products(box, inner, second, links, own, back, map_b, low, chirality)
    for s in range(box.count):
        update[s] = weight_a * field[s] + weight_b * second[s]
    for k in range(len(outer.tiles)):
        back_products(outer, k, update, links, back, chirality)
    for s in range(box.count):
        image[s] = weight_a * map_a[s] + weight_b * map_b[s]

    def aligned(s, d, side):
        piece, found = back_value(outer, (s, d), back, lanes)
        return piece if found == side else pltpu.roll(piece, half, 1)

    for d in range(4):
        flip = flips[d]
        lower = box.rim(d, False)
        upper = box.rim(d, True)
        for j in range(len(lower) // 4):
            block = []
            for k in (4 * j, 4 * j + 2):
                block.append(jnp.where(low, update[lower[k]], update[lower[k + 1]]))
            sends[d][flip, j] = jnp.concatenate(block, axis=0).astype(BF16)
            block = []
            for k in (4 * j, 4 * j + 2):
                joined = jnp.where(low, aligned(upper[k], d, 0), aligned(upper[k + 1], d, 1))
                block.append(chirality * joined)
            sends[d][1 - flip, j] = jnp.concatenate(block, axis=0).astype(BF16)


def first_kernel(box, parts, kinds, rhs_in, own_in, hop_in, *refs):
    flips = sent_slots(kinds)
    update, image, send0, send1, send2, send3, links, own = refs[:8]
    field, back, map_a, map_b, second, rhs, own_raw, hop, sems = refs[8:]
    each = box.count // parts
    copies = [pltpu.make_async_copy(rhs_in, rhs, sems.at[2 * parts])]
    for c in range(parts):
        run = pl.ds(c * each, each)
        copies.append(pltpu.make_async_copy(hop_in.at[:, run], hop.at[:, run], sems.at[2 * c]))
        copies.append(pltpu.make_async_copy(own_in.at[run], own_raw.at[run], sems.at[2 * c + 1]))
    for copy in copies:
        copy.start()
    copies[0].wait()
    for s in range(box.count):
        field[s] = twice(rhs[s])
    inner, outer = split_links(box)
    blank = jnp.zeros(hop.shape[2:], BF16)
    arrived = [0]
    packed = [0]

    def await_site(s):
        while arrived[0] * each <= s:
            c = arrived[0]
            copies[2 * c + 1].wait()
            copies[2 * c + 2].wait()
            arrived[0] += 1

    def pack(tiles, k):
        matrices = [hop[d, s] for s, d in tiles.tiles[k]]
        matrices += [blank] * (4 - len(matrices))
        links[tiles.first + k] = jnp.concatenate(matrices, axis=1)

    def prepare(group=None, tile=None):
        if group is not None:
            sites = range(GROUP * group, GROUP * group + GROUP)
            await_site(sites[-1])
            own[group] = jnp.concatenate([own_raw[s] for s in sites], axis=1)
        if tile is not None:
            await_site(inner.sites[tile][-1])
            pack(inner, tile)
            final = tile == len(inner.tiles) - 1
            if final:
                await_site(box.count - 1)
            while packed[0] < len(outer.tiles) and (final or outer.sites[packed[0]][-1] < arrived[0] * each):
                pack(outer, packed[0])
                packed[0] += 1
                if not final and packed[0] * len(inner.tiles) > (tile + 1) * len(outer.tiles):
                    break

    scratch = (back, map_a, map_b, second)
    smooth(box, flips, field, links, own, (update, image, (send0, send1, send2, send3)), scratch, prepare)


def second_kernel(box, kinds, rhs, mapped, sums, links, own, update, image, send0, send1, send2, send3, field, *scratch):
    flips = sent_slots(kinds)
    top, square = unpacked_sums(sums, 2, mapped.shape[1])
    alpha = top / square
    for s in range(box.count):
        field[s] = twice(rhs[s]) - alpha * mapped[s]
    smooth(box, flips, field, links, own, (update, image, (send0, send1, send2, send3)), scratch)


def joined_halo(box, flips, image, links, came, mapped, low):
    rows, lanes = image.shape[1:]
    half = lanes // 2

    places = [{s: k for k, s in enumerate(box.rim(d, True))} for d in range(4)]
    lows = [{s: k for k, s in enumerate(box.rim(d, False))} for d in range(4)]

    def read(d, which, k):
        slot = flips[d] if which == 0 else 1 - flips[d]
        tile = came[d][slot, k // 4].astype(F32)
        return tile[(k // 2 % 2) * rows : (k // 2 % 2 + 1) * rows]

    zero = jnp.zeros((rows, lanes), F32)
    _, outer = split_links(box)

    def value(s, d, slot):
        k = places[d][s]
        tile = read(d, 0, k)
        return tile if k % 2 == slot % 2 else pltpu.roll(tile, half, 1)

    parts = {}
    last = {}
    for k, sites in enumerate(outer.sites):
        for s in sites:
            last[s] = k

    def finish(s):
        extra = zero
        if s in parts:
            extra = jnp.concatenate([parts.pop(s), jnp.zeros((rows, half), F32)], axis=1)
        for d in range(4):
            if s in lows[d]:
                k = lows[d][s]
                tile = read(d, 1, k)
                extra = extra + (jnp.where(low, tile, 0.0) if k % 2 == 0 else jnp.where(low, 0.0, tile))
        mapped[s] = image[s] + extra + pltpu.roll(extra, half, 1)

    done = 0
    for k in range(len(outer.tiles)):
        for s, part in ahead_products(outer, k, value, links, low, zero).items():
            parts[s] = parts[s] + part if s in parts else part
        while done < box.count and last.get(done, -1) <= k - LAG:
            finish(done)
            done += 1
    for s in range(done, box.count):
        finish(s)


def sum_places(rows, lanes):
    row = lax.broadcasted_iota(jnp.int32, (rows, lanes), 0)
    lane = lax.broadcasted_iota(jnp.int32, (rows, lanes), 1)
    return lane - row


def packed_sums(values, out):
    rows, lanes = values[0].shape
    places = sum_places(rows, lanes)
    spread = jnp.zeros((rows, lanes), F32)
    for k, value in enumerate(values):
        spread = jnp.where(places == k * rows, jnp.sum(value, axis=1, keepdims=True), spread)
    out[...] = jnp.broadcast_to(jnp.sum(spread, axis=0, keepdims=True), out.shape)


def unpacked_sums(sums, count, rows):
    lanes = sums.shape[1]
    total = jnp.broadcast_to(jnp.sum(sums[...], axis=0, keepdims=True), (rows, lanes))
    places = sum_places(rows, lanes)
    return [
        jnp.sum(jnp.where(places == k * rows, total, 0.0), axis=1, keepdims=True) for k in range(count)
    ]


def third_kernel(box, kinds, rhs, image, links, came3, came2, came1, came0, mapped, sums):
    rows, lanes = image.shape[1:]
    low, _ = lane_tools(rows, lanes)
    joined_halo(box, came_slots(kinds), image, links, (came0, came1, came2, came3), mapped, low)
    zero = jnp.zeros((rows, lanes), F32)
    top = zero
    bottom = zero
    for s in range(box.count):
        value = mapped[s]
        top = top + value * twice(rhs[s])
        bottom = bottom + value * value
    packed_sums((top, bottom), sums)


def fourth_kernel(box, kinds, rhs, first, before, image, links, came3, came2, came1, came0, mapped, sums):
    rows, lanes = image.shape[1:]
    low, _ = lane_tools(rows, lanes)
    joined_halo(box, came_slots(kinds), image, links, (came0, came1, came2, came3), mapped, low)
    top, square = unpacked_sums(before, 2, rows)
    alpha = top / square
    total = [jnp.zeros((rows, lanes), F32) for _ in range(4)]
    for s in range(box.count):
        old = first[s]
        value = mapped[s]
        remain = twice(rhs[s]) - alpha * old
        for k, product in enumerate((old * value, value * value, value * remain, old * remain)):
            total[k] = total[k] + product
    packed_sums(total, sums)


def last_kernel(box, rhs, update_a, map_a, update_b, map_b, sums_a, sums_b, solution_out, residual_out):
    rows, lanes = update_a.shape[1:]
    half = lanes // 2
    top, square = unpacked_sums(sums_a, 2, rows)
    alpha = top / square
    cross, norm, raw, old = unpacked_sums(sums_b, 4, rows)
    beta = cross / square
    step = (raw - beta * old) / (norm - 2.0 * beta * cross + beta * beta * square)
    for s in range(box.count):
        old = update_a[s][:, :half]
        solution_out[s] = alpha * old + step * (update_b[s][:, :half] - beta * old)
        old = map_a[s][:, :half]
        residual_out[s] = rhs[s] - alpha * old - step * (map_b[s][:, :half] - beta * old)


def call(body, outs, scratch, ins, space=pltpu.VMEM):
    vmem = pl.BlockSpec(memory_space=pltpu.VMEM)
    return pl.pallas_call(
        body,
        out_shape=outs,
        in_specs=[pl.BlockSpec(memory_space=space)] * len(ins),
        out_specs=[vmem] * len(outs),
        scratch_shapes=scratch,
        compiler_params=pltpu.CompilerParams(vmem_limit_bytes=VMEM_BYTES),
    )(*ins)


def plan(direction):
    axis = AXES[direction]
    size = lax.axis_size(axis)
    step = min(8, max(2, lax.axis_size("gx") // 8)) if direction == 0 else 1
    if 2 * step % size == 0:
        return axis, size, step, "both"
    if step == 1 and size % 2 == 0:
        return axis, size, step, "pairs"
    return axis, size, step, "shift"


def message_tiles(box):
    tiles = [len(box.rim(d, True)) // 4 for d in range(4)]
    longest = 2 * max(tiles[:2])
    return tiles[:2] + [longest // 2 + 1, longest + 1]


def exchange(sends):
    came = [None] * 4
    for d in reversed(range(4)):
        axis, size, step, kind = plan(d)
        ring = range(size)
        if kind == "both":
            came[d] = lax.ppermute(sends[d], axis, [(i, (i + step) % size) for i in ring])
        elif kind == "pairs":
            even = lax.ppermute(sends[d][0], axis, [(i, i ^ 1) for i in ring])
            odd = lax.ppermute(sends[d][1], axis, [(i, (i + 1 if i % 2 else i - 1) % size) for i in ring])
            came[d] = jnp.stack([even, odd])
        else:
            field = lax.ppermute(sends[d][0], axis, [(i, (i - step) % size) for i in ring])
            back = lax.ppermute(sends[d][1], axis, [(i, (i + step) % size) for i in ring])
            came[d] = jnp.stack([field, back])
    return came


def device_count():
    return lax.axis_size("gx") * lax.axis_size("gz") * lax.axis_size("ta")


def sum_rows():
    return device_count() if device_count() <= 64 else 1


def mesh_sum(value):
    if sum_rows() > 1:
        return lax.all_to_all(value, ("gx", "gz", "ta"), 0, 0, tiled=True)
    for axis in ("gx", "gz", "ta"):
        size = lax.axis_size(axis)
        if size & (size - 1):
            value = lax.psum(value, axis)
            continue
        hop = 1
        while hop < size:
            value = value + lax.ppermute(value, axis, [(i, i ^ hop) for i in range(size)])
            hop *= 2
    return value


def on_device(rhs, self_coupling, hopping):
    extents = rhs.shape[1:5]
    rows, channels = rhs.shape[5:]
    lanes = 2 * channels
    box = Box(extents)
    count = box.count
    source = rhs.reshape(count, rows, channels)
    own = self_coupling.reshape(count, channels, channels)
    hop = hopping.reshape(4, count, channels, channels)

    kinds = [plan(d)[3] for d in range(4)]
    full = jax.ShapeDtypeStruct((count, rows, lanes), F32)
    small = jax.ShapeDtypeStruct((sum_rows(), lanes), F32)
    narrow = jax.ShapeDtypeStruct((count, rows, channels), F32)
    inner, outer = split_links(box)
    link_tiles = len(inner.tiles) + len(outer.tiles)
    links_shape = jax.ShapeDtypeStruct((link_tiles, channels, 4 * channels), BF16)
    own_shape = jax.ShapeDtypeStruct((count // GROUP, channels, GROUP * channels), BF16)
    parts = extents[0] * extents[1]
    raw = [
        pltpu.VMEM(source.shape, F32),
        pltpu.VMEM(own.shape, BF16),
        pltpu.VMEM(hop.shape, BF16),
        pltpu.SemaphoreType.DMA((2 * parts + 1,)),
    ]
    send_shapes = [
        jax.ShapeDtypeStruct((2, tiles, 2 * rows, lanes), BF16) for tiles in message_tiles(box)
    ]
    field_scratch = pltpu.VMEM((count, rows, lanes), F32)
    back_scratch = pltpu.VMEM((max(inner.runs, outer.runs), rows, 4 * channels), F32)
    scratch = [field_scratch, back_scratch, field_scratch, field_scratch, field_scratch]

    update_a, image_a, *sends, links, own = call(
        functools.partial(first_kernel, box, parts, kinds),
        [full, full, *send_shapes, links_shape, own_shape],
        scratch + raw,
        [pltpu.with_memory_space_constraint(a, pltpu.HBM) for a in (source, own, hop)],
        pltpu.HBM,
    )
    came = exchange(sends)
    map_a, sums_a = call(
        functools.partial(third_kernel, box, kinds), [full, small], [], (source, image_a, links, *came[::-1])
    )
    sums_a = mesh_sum(sums_a)
    update_b, image_b, *sends = call(
        functools.partial(second_kernel, box, kinds),
        [full, full, *send_shapes],
        scratch,
        (source, map_a, sums_a, links, own),
    )
    came = exchange(sends)
    map_b, sums_b = call(
        functools.partial(fourth_kernel, box, kinds),
        [full, small],
        [],
        (source, map_a, sums_a, image_b, links, *came[::-1]),
    )
    sums_b = mesh_sum(sums_b)
    found, left = call(
        functools.partial(last_kernel, box),
        [narrow, narrow],
        [],
        (source, update_a, map_a, update_b, map_b, sums_a, sums_b),
    )
    return found.reshape(rhs.shape), left.reshape(rhs.shape)


def solution(mesh):
    in_specs = (
        P("gx", None, None, "gz", "ta", None, None),
        P("gx", None, None, "gz", "ta", None, None),
        P(None, "gx", None, None, "gz", "ta", None, None),
    )
    out_specs = (
        P("gx", None, None, "gz", "ta", None, None),
        P("gx", None, None, "gz", "ta", None, None),
    )
    return jax.shard_map(
        on_device, mesh=mesh, in_specs=in_specs, out_specs=out_specs, check_vma=False
    )
```

```python
import functools

import jax
import jax.numpy as jnp
from jax import lax
from jax.experimental import pallas as pl
from jax.experimental.pallas import tpu as pltpu
from jax.sharding import PartitionSpec as P

F32 = jnp.float32
BF16 = jnp.bfloat16
NT = (((1,), (1,)), ((), ()))
NN = (((1,), (0,)), ((), ()))
VMEM_BYTES = 24 * 2**20
GROUP = 4
LAG = 4
AXES = ("gx", "gx", "gz", "ta")


class Box:
    def __init__(self, extents):
        self.extents = tuple(extents)
        self.strides = []
        count = 1
        for extent in reversed(self.extents):
            self.strides.insert(0, count)
            count *= extent
        self.count = count

    def coord(self, site, direction):
        return site // self.strides[direction] % self.extents[direction]

    def ahead(self, site, direction):
        last = self.extents[direction] - 1
        return None if self.coord(site, direction) == last else site + self.strides[direction]

    def behind(self, site, direction):
        return None if self.coord(site, direction) == 0 else site - self.strides[direction]

    def rim(self, direction, upper):
        wanted = self.extents[direction] - 1 if upper else 0
        return [s for s in range(self.count) if self.coord(s, direction) == wanted]


class Tiles:
    def __init__(self, blocks, first):
        self.first = first
        self.tiles = [blocks[k : k + 4] for k in range(0, len(blocks), 4)]
        self.sites = [list(dict.fromkeys(s for s, _ in tile)) for tile in self.tiles]
        self.starts = []
        self.place = {}
        self.runs = 0
        for tile, sites in zip(self.tiles, self.sites):
            self.starts.append(self.runs)
            for slot, block in enumerate(tile):
                self.place[block] = (self.runs + sites.index(block[0]), slot)
            self.runs += len(sites)


def split_links(box):
    blocks = [(s, d) for s in range(box.count) for d in range(4)]
    inner = Tiles([b for b in blocks if box.ahead(*b) is not None], 0)
    outer = Tiles([b for b in blocks if box.ahead(*b) is None], len(inner.tiles))
    return inner, outer


def slotted(contents, low, zero):
    halves = []
    for left, right in (contents[:2], contents[2:]):
        if left is None and right is None:
            halves.append(zero)
        else:
            halves.append(jnp.where(low, zero if left is None else left, zero if right is None else right))
    return jnp.concatenate(halves, axis=1)


def ahead_products(tiles, k, value, links, low, zero):
    rows = zero.shape[0]
    stack = []
    for s in tiles.sites[k]:
        contents = [value(s, d, slot) if t == s else None for slot, (t, d) in enumerate(tiles.tiles[k])]
        contents += [None] * (4 - len(contents))
        stack.append(slotted(contents, low, zero))
    spread = jnp.concatenate(stack, axis=0).astype(BF16)
    total = lax.dot_general(spread, links[tiles.first + k], NT, preferred_element_type=F32)
    return {s: total[i * rows : (i + 1) * rows] for i, s in enumerate(tiles.sites[k])}


def back_products(tiles, k, field, links, back, chirality):
    rows, lanes = field.shape[1:]
    stack = jnp.concatenate([chirality * field[s] for s in tiles.sites[k]], axis=0)
    product = lax.dot_general(
        stack[:, : lanes // 2].astype(BF16), links[tiles.first + k], NN, preferred_element_type=F32
    )
    for i in range(len(tiles.sites[k])):
        back[tiles.starts[k] + i] = product[i * rows : (i + 1) * rows]


def back_value(tiles, block, back, lanes):
    run, slot = tiles.place[block]
    return back[run, :, slot // 2 * lanes : (slot // 2 + 1) * lanes], slot % 2


def lane_tools(rows, lanes):
    lane = lax.broadcasted_iota(jnp.int32, (rows, lanes), 1)
    low = lane < lanes // 2
    chirality = jnp.where(lane % (lanes // 2) < lanes // 4, 1.0, -1.0).astype(F32)
    return low, chirality


def twice(value):
    return jnp.concatenate([value, value], axis=1)


def own_products(group, here, own, low):
    rows, lanes = here[0].shape
    zero = jnp.zeros((rows, lanes), F32)
    left = [jnp.where(low, here[0], 0.0), jnp.where(low, 0.0, here[1]), zero, zero]
    right = [zero, zero, jnp.where(low, here[2], 0.0), jnp.where(low, 0.0, here[3])]
    blocks = jnp.concatenate(
        [jnp.concatenate(left, axis=0), jnp.concatenate(right, axis=0)], axis=1
    ).astype(BF16)
    return lax.dot_general(blocks, own[group], NT, preferred_element_type=F32)


def local_products(box, tiles, field, links, own, back, mapped, low, chirality, prepare=None):
    rows, lanes = field.shape[1:]
    half = lanes // 2
    zero = jnp.zeros((rows, lanes), F32)
    top = [zero]
    bottom = [zero]
    parts = {}

    def value(s, d, _):
        return field[box.ahead(s, d)]

    def diagonal(g):
        if prepare is not None:
            prepare(group=g)
        sites = range(GROUP * g, GROUP * g + GROUP)
        total = own_products(g, [field[s] for s in sites], own, low)
        for i, s in enumerate(sites):
            parts[s] = total[i * rows : (i + 1) * rows]

    def gather(s):
        sums = [None, None]
        for d in range(4):
            b = box.behind(s, d)
            if b is not None:
                piece, side = back_value(tiles, (b, d), back, lanes)
                sums[side] = piece if sums[side] is None else sums[side] + piece
        gathered = mapped[s]
        if sums[0] is not None or sums[1] is not None:
            sums = [zero if x is None else x for x in sums]
            gathered = chirality * jnp.where(low, sums[0], sums[1]) + gathered
        here = field[s]
        result = 4.0 * here + gathered + pltpu.roll(gathered, half, 1)
        mapped[s] = result
        top[0] = top[0] + result * here
        bottom[0] = bottom[0] + result * result

    last = {}
    for k, sites in enumerate(tiles.sites):
        for s in sites:
            last[s] = k
    ready = 0
    done = 0
    for k in range(len(tiles.tiles) + LAG):
        if k < len(tiles.tiles):
            for s in tiles.sites[k]:
                while ready * GROUP <= s:
                    diagonal(ready)
                    ready += 1
            if prepare is not None:
                prepare(tile=k)
            for s, part in ahead_products(tiles, k, value, links, low, zero).items():
                parts[s] = parts[s] + part
            back_products(tiles, k, field, links, back, chirality)
            for s in tiles.sites[k]:
                if last[s] == k:
                    mapped[s] = jnp.concatenate([parts.pop(s), jnp.zeros((rows, half), F32)], axis=1)
        if k >= LAG:
            while done < box.count and last.get(done, -1) <= k - LAG and done // GROUP < ready:
                if done in parts:
                    mapped[done] = jnp.concatenate([parts.pop(done), jnp.zeros((rows, half), F32)], axis=1)
                gather(done)
                done += 1
    while ready * GROUP < box.count:
        diagonal(ready)
        ready += 1
    while done < box.count:
        if done in parts:
            mapped[done] = jnp.concatenate([parts.pop(done), jnp.zeros((rows, half), F32)], axis=1)
        gather(done)
        done += 1
    return jnp.sum(top[0], axis=1, keepdims=True) / jnp.sum(bottom[0], axis=1, keepdims=True)


def came_slots(kinds):
    return [lax.axis_index(AXES[d]) % 2 if kinds[d] == "pairs" else 0 for d in range(4)]


def sent_slots(kinds):
    return [1 - slot if kind == "pairs" else 0 for kind, slot in zip(kinds, came_slots(kinds))]


def smooth(box, flips, field, links, own, outs, scratch, prepare=None):
    update, image, sends = outs
    back, map_a, map_b, second = scratch
    rows, lanes = field.shape[1:]
    half = lanes // 2
    low, chirality = lane_tools(rows, lanes)
    inner, outer = split_links(box)
    weight_a = local_products(box, inner, field, links, own, back, map_a, low, chirality, prepare)
    for s in range(box.count):
        second[s] = field[s] - weight_a * map_a[s]
    weight_b = local_products(box, inner, second, links, own, back, map_b, low, chirality)
    for s in range(box.count):
        update[s] = weight_a * field[s] + weight_b * second[s]
    for k in range(len(outer.tiles)):
        back_products(outer, k, update, links, back, chirality)
    for s in range(box.count):
        image[s] = weight_a * map_a[s] + weight_b * map_b[s]

    def aligned(s, d, side):
        piece, found = back_value(outer, (s, d), back, lanes)
        return piece if found == side else pltpu.roll(piece, half, 1)

    for d in range(4):
        flip = flips[d]
        lower = box.rim(d, False)
        upper = box.rim(d, True)
        for j in range(len(lower) // 4):
            block = []
            for k in (4 * j, 4 * j + 2):
                block.append(jnp.where(low, update[lower[k]], update[lower[k + 1]]))
            sends[d][flip, j] = jnp.concatenate(block, axis=0).astype(BF16)
            block = []
            for k in (4 * j, 4 * j + 2):
                joined = jnp.where(low, aligned(upper[k], d, 0), aligned(upper[k + 1], d, 1))
                block.append(chirality * joined)
            sends[d][1 - flip, j] = jnp.concatenate(block, axis=0).astype(BF16)


def first_kernel(box, parts, kinds, rhs_in, own_in, hop_in, *refs):
    flips = sent_slots(kinds)
    update, image, send0, send1, send2, send3, links, own = refs[:8]
    field, back, map_a, map_b, second, rhs, own_raw, hop, sems = refs[8:]
    groups = box.count // GROUP
    bounds = [0, GROUP * (groups // 4), GROUP * (groups * 5 // 8), box.count]
    copies = [pltpu.make_async_copy(rhs_in, rhs, sems.at[2 * parts])]
    for c in range(parts):
        run = pl.ds(bounds[c], bounds[c + 1] - bounds[c])
        copies.append(pltpu.make_async_copy(hop_in.at[:, run], hop.at[:, run], sems.at[2 * c]))
        copies.append(pltpu.make_async_copy(own_in.at[run], own_raw.at[run], sems.at[2 * c + 1]))
    for copy in copies:
        copy.start()
    copies[0].wait()
    for s in range(box.count):
        field[s] = twice(rhs[s])
    inner, outer = split_links(box)
    blank = jnp.zeros(hop.shape[2:], BF16)
    arrived = [0]
    packed = [0]

    def await_site(s):
        while bounds[arrived[0]] <= s:
            c = arrived[0]
            copies[2 * c + 1].wait()
            copies[2 * c + 2].wait()
            arrived[0] += 1

    def pack(tiles, k):
        matrices = [hop[d, s] for s, d in tiles.tiles[k]]
        matrices += [blank] * (4 - len(matrices))
        links[tiles.first + k] = jnp.concatenate(matrices, axis=1)

    def prepare(group=None, tile=None):
        if group is not None:
            sites = range(GROUP * group, GROUP * group + GROUP)
            await_site(sites[-1])
            own[group] = jnp.concatenate([own_raw[s] for s in sites], axis=1)
        if tile is not None:
            await_site(inner.sites[tile][-1])
            pack(inner, tile)
            final = tile == len(inner.tiles) - 1
            if final:
                await_site(box.count - 1)
            while packed[0] < len(outer.tiles) and (final or outer.sites[packed[0]][-1] < bounds[arrived[0]]):
                pack(outer, packed[0])
                packed[0] += 1
                if not final and packed[0] * len(inner.tiles) > (tile + 1) * len(outer.tiles):
                    break

    scratch = (back, map_a, map_b, second)
    smooth(box, flips, field, links, own, (update, image, (send0, send1, send2, send3)), scratch, prepare)


def second_kernel(box, kinds, rhs, mapped, sums, links, own, update, image, send0, send1, send2, send3, field, *scratch):
    flips = sent_slots(kinds)
    top, square = unpacked_sums(sums, 2, mapped.shape[1])
    alpha = top / square
    for s in range(box.count):
        field[s] = twice(rhs[s]) - alpha * mapped[s]
    smooth(box, flips, field, links, own, (update, image, (send0, send1, send2, send3)), scratch)


def joined_halo(box, flips, image, links, came, mapped, low):
    rows, lanes = image.shape[1:]
    half = lanes // 2

    places = [{s: k for k, s in enumerate(box.rim(d, True))} for d in range(4)]
    lows = [{s: k for k, s in enumerate(box.rim(d, False))} for d in range(4)]

    def read(d, which, k):
        slot = flips[d] if which == 0 else 1 - flips[d]
        tile = came[d][slot, k // 4].astype(F32)
        return tile[(k // 2 % 2) * rows : (k // 2 % 2 + 1) * rows]

    zero = jnp.zeros((rows, lanes), F32)
    _, outer = split_links(box)

    def value(s, d, slot):
        k = places[d][s]
        tile = read(d, 0, k)
        return tile if k % 2 == slot % 2 else pltpu.roll(tile, half, 1)

    parts = {}
    last = {}
    for k, sites in enumerate(outer.sites):
        for s in sites:
            last[s] = k

    def finish(s):
        extra = zero
        if s in parts:
            extra = jnp.concatenate([parts.pop(s), jnp.zeros((rows, half), F32)], axis=1)
        for d in range(4):
            if s in lows[d]:
                k = lows[d][s]
                tile = read(d, 1, k)
                extra = extra + (jnp.where(low, tile, 0.0) if k % 2 == 0 else jnp.where(low, 0.0, tile))
        mapped[s] = image[s] + extra + pltpu.roll(extra, half, 1)

    done = 0
    for k in range(len(outer.tiles)):
        for s, part in ahead_products(outer, k, value, links, low, zero).items():
            parts[s] = parts[s] + part if s in parts else part
        while done < box.count and last.get(done, -1) <= k - LAG:
            finish(done)
            done += 1
    for s in range(done, box.count):
        finish(s)


def sum_places(rows, lanes):
    row = lax.broadcasted_iota(jnp.int32, (rows, lanes), 0)
    lane = lax.broadcasted_iota(jnp.int32, (rows, lanes), 1)
    return lane - row


def packed_sums(values, out):
    rows, lanes = values[0].shape
    places = sum_places(rows, lanes)
    spread = jnp.zeros((rows, lanes), F32)
    for k, value in enumerate(values):
        spread = jnp.where(places == k * rows, jnp.sum(value, axis=1, keepdims=True), spread)
    out[...] = jnp.broadcast_to(jnp.sum(spread, axis=0, keepdims=True), out.shape)


def unpacked_sums(sums, count, rows):
    lanes = sums.shape[1]
    total = jnp.broadcast_to(jnp.sum(sums[...], axis=0, keepdims=True), (rows, lanes))
    places = sum_places(rows, lanes)
    return [
        jnp.sum(jnp.where(places == k * rows, total, 0.0), axis=1, keepdims=True) for k in range(count)
    ]


def third_kernel(box, kinds, rhs, image, links, came3, came2, came1, came0, mapped, sums):
    rows, lanes = image.shape[1:]
    low, _ = lane_tools(rows, lanes)
    joined_halo(box, came_slots(kinds), image, links, (came0, came1, came2, came3), mapped, low)
    zero = jnp.zeros((rows, lanes), F32)
    top = zero
    bottom = zero
    for s in range(box.count):
        value = mapped[s]
        top = top + value * twice(rhs[s])
        bottom = bottom + value * value
    packed_sums((top, bottom), sums)


def fourth_kernel(box, kinds, rhs, first, before, image, links, came3, came2, came1, came0, mapped, sums):
    rows, lanes = image.shape[1:]
    low, _ = lane_tools(rows, lanes)
    joined_halo(box, came_slots(kinds), image, links, (came0, came1, came2, came3), mapped, low)
    top, square = unpacked_sums(before, 2, rows)
    alpha = top / square
    total = [jnp.zeros((rows, lanes), F32) for _ in range(4)]
    for s in range(box.count):
        old = first[s]
        value = mapped[s]
        remain = twice(rhs[s]) - alpha * old
        for k, product in enumerate((old * value, value * value, value * remain, old * remain)):
            total[k] = total[k] + product
    packed_sums(total, sums)


def last_kernel(box, rhs, update_a, map_a, update_b, map_b, sums_a, sums_b, solution_out, residual_out):
    rows, lanes = update_a.shape[1:]
    half = lanes // 2
    top, square = unpacked_sums(sums_a, 2, rows)
    alpha = top / square
    cross, norm, raw, old = unpacked_sums(sums_b, 4, rows)
    beta = cross / square
    step = (raw - beta * old) / (norm - 2.0 * beta * cross + beta * beta * square)
    for s in range(box.count):
        old = update_a[s][:, :half]
        solution_out[s] = alpha * old + step * (update_b[s][:, :half] - beta * old)
        old = map_a[s][:, :half]
        residual_out[s] = rhs[s] - alpha * old - step * (map_b[s][:, :half] - beta * old)


def call(body, outs, scratch, ins, space=pltpu.VMEM):
    vmem = pl.BlockSpec(memory_space=pltpu.VMEM)
    return pl.pallas_call(
        body,
        out_shape=outs,
        in_specs=[pl.BlockSpec(memory_space=space)] * len(ins),
        out_specs=[vmem] * len(outs),
        scratch_shapes=scratch,
        compiler_params=pltpu.CompilerParams(vmem_limit_bytes=VMEM_BYTES),
    )(*ins)


def plan(direction):
    axis = AXES[direction]
    size = lax.axis_size(axis)
    step = min(8, max(2, lax.axis_size("gx") // 8)) if direction == 0 else 1
    if 2 * step % size == 0:
        return axis, size, step, "both"
    if step == 1 and size % 2 == 0:
        return axis, size, step, "pairs"
    return axis, size, step, "shift"


def message_tiles(box):
    tiles = [len(box.rim(d, True)) // 4 for d in range(4)]
    longest = 2 * max(tiles[:2])
    return tiles[:2] + [longest // 2 + 1, longest + 1]


def exchange(sends):
    came = [None] * 4
    for d in reversed(range(4)):
        axis, size, step, kind = plan(d)
        ring = range(size)
        if kind == "both":
            came[d] = lax.ppermute(sends[d], axis, [(i, (i + step) % size) for i in ring])
        elif kind == "pairs":
            even = lax.ppermute(sends[d][0], axis, [(i, i ^ 1) for i in ring])
            odd = lax.ppermute(sends[d][1], axis, [(i, (i + 1 if i % 2 else i - 1) % size) for i in ring])
            came[d] = jnp.stack([even, odd])
        else:
            field = lax.ppermute(sends[d][0], axis, [(i, (i - step) % size) for i in ring])
            back = lax.ppermute(sends[d][1], axis, [(i, (i + step) % size) for i in ring])
            came[d] = jnp.stack([field, back])
    return came


def device_count():
    return lax.axis_size("gx") * lax.axis_size("gz") * lax.axis_size("ta")


def sum_rows():
    return device_count() if device_count() <= 64 else 1


def mesh_sum(value):
    if sum_rows() > 1:
        return lax.all_to_all(value, ("gx", "gz", "ta"), 0, 0, tiled=True)
    for axis in ("gx", "gz", "ta"):
        size = lax.axis_size(axis)
        if size & (size - 1):
            value = lax.psum(value, axis)
            continue
        hop = 1
        while hop < size:
            value = value + lax.ppermute(value, axis, [(i, i ^ hop) for i in range(size)])
            hop *= 2
    return value


def on_device(rhs, self_coupling, hopping):
    extents = rhs.shape[1:5]
    rows, channels = rhs.shape[5:]
    lanes = 2 * channels
    box = Box(extents)
    count = box.count
    source = rhs.reshape(count, rows, channels)
    own = self_coupling.reshape(count, channels, channels)
    hop = hopping.reshape(4, count, channels, channels)

    kinds = [plan(d)[3] for d in range(4)]
    full = jax.ShapeDtypeStruct((count, rows, lanes), F32)
    small = jax.ShapeDtypeStruct((sum_rows(), lanes), F32)
    narrow = jax.ShapeDtypeStruct((count, rows, channels), F32)
    inner, outer = split_links(box)
    link_tiles = len(inner.tiles) + len(outer.tiles)
    links_shape = jax.ShapeDtypeStruct((link_tiles, channels, 4 * channels), BF16)
    own_shape = jax.ShapeDtypeStruct((count // GROUP, channels, GROUP * channels), BF16)
    parts = 3
    raw = [
        pltpu.VMEM(source.shape, F32),
        pltpu.VMEM(own.shape, BF16),
        pltpu.VMEM(hop.shape, BF16),
        pltpu.SemaphoreType.DMA((2 * parts + 1,)),
    ]
    send_shapes = [
        jax.ShapeDtypeStruct((2, tiles, 2 * rows, lanes), BF16) for tiles in message_tiles(box)
    ]
    field_scratch = pltpu.VMEM((count, rows, lanes), F32)
    back_scratch = pltpu.VMEM((max(inner.runs, outer.runs), rows, 4 * channels), F32)
    scratch = [field_scratch, back_scratch, field_scratch, field_scratch, field_scratch]

    update_a, image_a, *sends, links, own = call(
        functools.partial(first_kernel, box, parts, kinds),
        [full, full, *send_shapes, links_shape, own_shape],
        scratch + raw,
        [pltpu.with_memory_space_constraint(a, pltpu.HBM) for a in (source, own, hop)],
        pltpu.HBM,
    )
    came = exchange(sends)
    map_a, sums_a = call(
        functools.partial(third_kernel, box, kinds), [full, small], [], (source, image_a, links, *came[::-1])
    )
    sums_a = mesh_sum(sums_a)
    update_b, image_b, *sends = call(
        functools.partial(second_kernel, box, kinds),
        [full, full, *send_shapes],
        scratch,
        (source, map_a, sums_a, links, own),
    )
    came = exchange(sends)
    map_b, sums_b = call(
        functools.partial(fourth_kernel, box, kinds),
        [full, small],
        [],
        (source, map_a, sums_a, image_b, links, *came[::-1]),
    )
    sums_b = mesh_sum(sums_b)
    found, left = call(
        functools.partial(last_kernel, box),
        [narrow, narrow],
        [],
        (source, update_a, map_a, update_b, map_b, sums_a, sums_b),
    )
    return found.reshape(rhs.shape), left.reshape(rhs.shape)


def solution(mesh):
    in_specs = (
        P("gx", None, None, "gz", "ta", None, None),
        P("gx", None, None, "gz", "ta", None, None),
        P(None, "gx", None, None, "gz", "ta", None, None),
    )
    out_specs = (
        P("gx", None, None, "gz", "ta", None, None),
        P("gx", None, None, "gz", "ta", None, None),
    )
    return jax.shard_map(
        on_device, mesh=mesh, in_specs=in_specs, out_specs=out_specs, check_vma=False
    )
```
